32 devices in a mesh: dp: 2 (over core), ctx: 8 (over z, y), fsdp: 2 (over x).
Axes of the slice: x: 2, y: 2, z: 4, core: 2. Of those that a mesh axis runs over, the one named last changes fastest.
Arguments:
- tokens: bfloat16 [4, 2048, 1024], P(('dp', 'fsdp'), 'ctx'), may hold values from -6 to 6
- segment_ids: int32 [4, 2048], P(('dp', 'fsdp'), 'ctx'), may hold values from 0 to 15, never falling along the last dimension, each value on 1 to 1280 neighbouring positions
- w_query: bfloat16 [1024, 1024], P(('ctx', 'fsdp')), may hold values from -0.1875 to 0.1875
- b_query: bfloat16 [1024], P(('ctx', 'fsdp')), may hold values from -3 to 3
- w_key: bfloat16 [1024, 1024], P(('ctx', 'fsdp')), may hold values from -0.1875 to 0.1875
- w_value: bfloat16 [1024, 1024], P(('ctx', 'fsdp')), may hold values from -0.1875 to 0.1875
- b_value: bfloat16 [1024], P(('ctx', 'fsdp')), may hold values from -3 to 3
- w_out: bfloat16 [1024, 1024], P(('ctx', 'fsdp')), may hold values from -1.5 to 1.5
- b_out: bfloat16 [1024], P(('ctx', 'fsdp')), may hold values from -3 to 3
- g_attn: bfloat16 [1024], P(('ctx', 'fsdp')), may hold values from 0.5 to 1.5
- n_attn: bfloat16 [1024], P(('ctx', 'fsdp')), may hold values from -3 to 3
- w_in: bfloat16 [1024, 4096], P(('ctx', 'fsdp')), may hold values from -0.1875 to 0.1875
- b_in: bfloat16 [4096], P(('ctx', 'fsdp')), may hold values from -3 to 3
- w_back: bfloat16 [4096, 1024], P(('ctx', 'fsdp')), may hold values from -0.09375 to 0.09375
- b_back: bfloat16 [1024], P(('ctx', 'fsdp')), may hold values from -3 to 3
- g_ffn: bfloat16 [1024], P(('ctx', 'fsdp')), may hold values from 0.5 to 1.5
- n_ffn: bfloat16 [1024], P(('ctx', 'fsdp')), may hold values from -3 to 3
- cotangent: bfloat16 [4, 2048, 1024], P(('dp', 'fsdp'), 'ctx'), may hold values from -6 to 6
Outputs:
- output: bfloat16 [4, 2048, 1024], P(('dp', 'fsdp'), 'ctx')
- grad_tokens: float32 [4, 2048, 1024], P(('dp', 'fsdp'), 'ctx')
- grad_w_query: float32 [1024, 1024], P(('ctx', 'fsdp'))
- grad_b_query: float32 [1024], P(('ctx', 'fsdp'))
- grad_w_key: float32 [1024, 1024], P(('ctx', 'fsdp'))
- grad_w_value: float32 [1024, 1024], P(('ctx', 'fsdp'))
- grad_b_value: float32 [1024], P(('ctx', 'fsdp'))
- grad_w_out: float32 [1024, 1024], P(('ctx', 'fsdp'))
- grad_b_out: float32 [1024], P(('ctx', 'fsdp'))
- grad_g_attn: float32 [1024], P(('ctx', 'fsdp'))
- grad_n_attn: float32 [1024], P(('ctx', 'fsdp'))
- grad_w_in: float32 [1024, 4096], P(('ctx', 'fsdp'))
- grad_b_in: float32 [4096], P(('ctx', 'fsdp'))
- grad_w_back: float32 [4096, 1024], P(('ctx', 'fsdp'))
- grad_b_back: float32 [1024], P(('ctx', 'fsdp'))
- grad_g_ffn: float32 [1024], P(('ctx', 'fsdp'))
- grad_n_ffn: float32 [1024], P(('ctx', 'fsdp'))
The draws below stay inside these ranges and needn't reach their ends.
Inputs may be any that keep to these rules, and one draw needn't show every extreme that they name: `segment_ids`: along a sequence the ids never fall; each of the 16 ids names 1 to 1280 consecutive tokens, and some document has exactly 1280 tokens.
All inputs are finite; a program needn't handle non-finite values.
Results may differ from the reference program's by a relative error of at most 0.017.
Values may be sent and summed in bfloat16 or wider, within the bound.
No kernel may reach another device: no remote copies, remote signals or barrier semaphores. Data moves between devices by JAX's collectives and lax.ppermute only.
A program may use at most 192 MiB of HBM per device.

```python
import math
import jax
import jax.numpy as jnp
import numpy as np
from jax import lax

D = 1024
H = 16
HD = 64
FF = 4096
DOCS = 16
SEQ_LEN = 2048
SEQS = 4
MOST_DOC = 1280


def block_scale(key, shape, shards, low, high):
    def one(position, parts):
        heights = jax.random.uniform(jax.random.fold_in(jax.random.fold_in(key, 6), position), (parts,), jnp.float32, low / len(shards), high / len(shards))
        return jnp.repeat(jnp.exp(heights), shape[position] // parts).reshape((-1,) + (1,) * (len(shape) - position - 1))

    gain = one(*shards[0])
    for cut in shards[1:]:
        gain = gain * one(*cut)
    return gain


def split_up(count, total, bound, skew):
    weights = [(1 << 20) // math.isqrt(rank ** skew) + 1 for rank in range(2, count + 1)]
    surplus, given = total - bound - (count - 1), [1] * (count - 1)
    while surplus > 0:
        movable = [i for i in range(count - 1) if given[i] < bound]
        whole, remaining = sum([weights[i] for i in movable]), surplus
        for i in movable:
            addition = min(bound - given[i], max(1, remaining * weights[i] // whole), surplus)
            given[i] = given[i] + addition
            surplus = surplus - addition
    return np.array([bound] + given)


def uneven(rng, count, total, bound, lean):
    if count == 2:
        one = jax.random.randint(rng, (), max(1, total - bound), min(bound, total - 1) + 1)
        return jnp.stack([one, total - one])
    lengths = jnp.asarray(split_up(count, total, bound, lean), jnp.int32)
    pairs = (count - 1) // 2
    source_of, taker = lengths[1:1 + 2 * pairs:2], lengths[2:2 + 2 * pairs:2]
    slack = jnp.minimum(source_of - 1, bound - taker)
    shifted = jax.random.randint(jax.random.fold_in(rng, 1), (pairs,), 0, 1 << 20) % (slack + 1)
    lengths = lengths.at[1:1 + 2 * pairs:2].set(source_of - shifted).at[2:2 + 2 * pairs:2].set(taker + shifted)
    return lengths[jax.random.permutation(jax.random.fold_in(rng, 2), count)]


def normal_values(rng, dims, spread, bound, cuts=(), dtype=jnp.bfloat16):
    loudness = block_scale(rng, dims, cuts, -0.22, 0.18) if cuts else 1.0
    drawn = jax.random.normal(rng, dims, jnp.float32) * spread * loudness
    return jnp.minimum(jnp.maximum(drawn, -bound), bound).astype(dtype)


def setup_inputs(seed: int = 0) -> dict:
    seeds = jax.random.split(jax.random.key(seed), 19)
    return {
        "tokens": normal_values(seeds[0], (SEQS, SEQ_LEN, D), 1.0, 6.0, ((0, 4), (1, 8))),
        "segment_ids": jax.vmap(lambda own: jnp.searchsorted(jnp.cumsum(uneven(own, DOCS, SEQ_LEN, MOST_DOC, 2)), jnp.arange(SEQ_LEN), side="right"))(jax.random.split(seeds[1], SEQS)).reshape((SEQS, SEQ_LEN)).astype(jnp.int32),
        "w_query": normal_values(seeds[2], (D, D), D ** -0.5, 0.1875, ((0, 16),)),
        "b_query": normal_values(seeds[3], (D,), 0.5, 3.0, ((0, 16),)),
        "w_key": normal_values(seeds[4], (D, D), D ** -0.5, 0.1875, ((0, 16),)),
        "w_value": normal_values(seeds[5], (D, D), D ** -0.5, 0.1875, ((0, 16),)),
        "b_value": normal_values(seeds[6], (D,), 0.5, 3.0, ((0, 16),)),
        "w_out": normal_values(seeds[7], (D, D), (D // 64) ** -0.5, 1.5, ((0, 16),)),
        "b_out": normal_values(seeds[8], (D,), 0.5, 3.0, ((0, 16),)),
        "g_attn": jnp.clip(1.0 + 0.1 * jax.random.normal(seeds[9], (D,), jnp.float32), 0.5, 1.5).astype(jnp.bfloat16),
        "n_attn": normal_values(seeds[10], (D,), 0.5, 3.0, ((0, 16),)),
        "w_in": normal_values(seeds[11], (D, FF), D ** -0.5, 0.1875, ((0, 16),)),
        "b_in": normal_values(seeds[12], (FF,), 0.5, 3.0, ((0, 16),)),
        "w_back": normal_values(seeds[13], (FF, D), FF ** -0.5, 0.09375, ((0, 16),)),
        "b_back": normal_values(seeds[14], (D,), 0.5, 3.0, ((0, 16),)),
        "g_ffn": jnp.clip(1.0 + 0.1 * jax.random.normal(seeds[15], (D,), jnp.float32), 0.5, 1.5).astype(jnp.bfloat16),
        "n_ffn": normal_values(seeds[16], (D,), 0.5, 3.0, ((0, 16),)),
        "cotangent": normal_values(seeds[17], (SEQS, SEQ_LEN, D), 1.0, 6.0, ((0, 4), (1, 8))),
    }


HIGH = lax.Precision.HIGHEST
NORM_EPS = 1e-05
NEG_FILL = -1e+30

@jax.custom_vjp
def low(v):
    return lax.optimization_barrier(v.astype(jnp.bfloat16)).astype(jnp.float32)

@jax.custom_vjp
def low_back(v):
    return v

def low_keep(v):
    return (low(v), None)

def low_pass(kept, upstream_gradient):
    return (upstream_gradient,)

def back_keep(v):
    return (v, None)

def back_low(kept, upstream_gradient):
    return (low(upstream_gradient),)
low.defvjp(low_keep, low_pass)
low_back.defvjp(back_keep, back_low)

def matmul(left, right):
    return jnp.dot(left, right, precision=HIGH)

def layer_norm(hidden, norm_gain, norm_shift):
    centered_input = hidden - lax.optimization_barrier(jnp.mean(hidden, -1, keepdims=True))
    inverse_deviation = lax.rsqrt(lax.optimization_barrier(jnp.mean(centered_input * centered_input, -1, keepdims=True)) + NORM_EPS)
    return centered_input * inverse_deviation * norm_gain + norm_shift

def attend_block(query_block, marks_block, key_rows, value_rows, doc_marks):
    block_rows = query_block.shape[0]
    heads_q = query_block.reshape(block_rows, H, HD)
    heads_k = key_rows.reshape(-1, H, HD)
    heads_v = value_rows.reshape(-1, H, HD)
    scores = low_back(jnp.einsum('thd,khd->htk', heads_q, heads_k, precision=HIGH) * (1.0 / math.sqrt(HD)))
    same_doc = marks_block[:, None] == doc_marks[None, :]
    logits = jnp.where(same_doc[None], scores, NEG_FILL)
    row_max = lax.optimization_barrier(jnp.max(logits, -1, keepdims=True))
    exp_block = jnp.exp(logits - row_max)
    probs_low = low(exp_block / lax.optimization_barrier(jnp.sum(exp_block, -1, keepdims=True)))
    return jnp.einsum('htk,khd->thd', probs_low, heads_v, precision=HIGH).reshape(block_rows, D)

def one_sequence(inputs, doc_marks, params):
    query_mat, query_bias, key_mat, value_mat, value_bias, out_mat, out_bias, attention_norm_gain, attn_shift, in_mat, in_bias, back_mat, back_bias, feedforward_norm_gain, feedforward_norm_shift = params
    query_rows = low(low_back(matmul(inputs, query_mat) + query_bias))
    key_rows = low(low_back(matmul(inputs, key_mat)))
    value_rows = low(low_back(matmul(inputs, value_mat) + value_bias))
    block_rows = min(512, SEQ_LEN)
    blocks = SEQ_LEN // block_rows
    attend = jax.checkpoint(attend_block)

    def per_block(block_pair):
        return attend(block_pair[0], block_pair[1], key_rows, value_rows, doc_marks)
    attended = lax.map(per_block, (query_rows.reshape(blocks, block_rows, D), doc_marks.reshape(blocks, block_rows)))
    attended = low(low_back(attended.reshape(SEQ_LEN, D)))
    branch = low_back(matmul(attended, out_mat) + out_bias)
    normalized_rows = layer_norm(inputs + branch, attention_norm_gain, attn_shift)
    inner = low_back(matmul(low(normalized_rows), in_mat) + in_bias)
    active = low(jax.nn.gelu(inner, approximate=False))
    feedforward_output = low_back(matmul(active, back_mat) + back_bias)
    return layer_norm(normalized_rows + feedforward_output, feedforward_norm_gain, feedforward_norm_shift)

def reference(tokens, segment_ids, w_query, b_query, w_key, w_value, b_value, w_out, b_out, g_attn, n_attn, w_in, b_in, w_back, b_back, g_ffn, n_ffn, cotangent):
    params = tuple((item.astype(jnp.float32) for item in (w_query, b_query, w_key, w_value, b_value, w_out, b_out, g_attn, n_attn, w_in, b_in, w_back, b_back, g_ffn, n_ffn)))

    def forward(inputs, weights):

        def per_sequence(item):
            return one_sequence(item[0], item[1], weights)
        return lax.map(per_sequence, (inputs, segment_ids))
    norm_result, pullback = jax.vjp(forward, tokens.astype(jnp.float32), params)
    grad_inputs, grad_params = pullback(cotangent.astype(jnp.float32))
    return (norm_result.astype(jnp.bfloat16), grad_inputs, grad_params[0], grad_params[1], grad_params[2], grad_params[3], grad_params[4], grad_params[5], grad_params[6], grad_params[7], grad_params[8], grad_params[9], grad_params[10], grad_params[11], grad_params[12], grad_params[13], grad_params[14])
```

```python
from functools import partial

import jax
import jax.numpy as jnp
import numpy as np
from jax import lax
from jax.experimental import pallas as pl
from jax.experimental.pallas import tpu as pltpu
from jax.sharding import PartitionSpec as P

D = 1024
H = 16
HD = 64
FF = 4096
NORM_EPS = 1e-05
NEG_FILL = -1e30
AXES = ("dp", "ctx", "fsdp")
BF = jnp.bfloat16
F32 = jnp.float32
VMEM_LIMIT = 48 * 1024 * 1024


def subset_masks(order):
    table = [0]
    for mask in order:
        table = table + [mask ^ entry for entry in table]
    return table


def bits_of(count):
    return [1 << t for t in range(count.bit_length() - 1)]


class Plan:
    def __init__(self, mesh):
        self.ctx = mesh.shape["ctx"]
        self.fsdp = mesh.shape["fsdp"]
        self.chips = self.ctx * self.fsdp
        self.groups = self.ctx // 2
        self.heads = H // self.ctx
        self.devices = [
            (c, j, f) for c in range(2) for j in range(self.ctx) for f in range(self.fsdp)
        ]
        bits = bits_of(self.chips)
        self.chip_orders = [bits[2:] + [1, 2], bits[2:] + [2, 1]]
        self.chip_masks = [subset_masks(order) for order in self.chip_orders]
        group_bits = bits_of(self.groups)
        self.group_orders = [group_bits[::-1], group_bits]
        self.group_masks = [subset_masks(order) for order in self.group_orders]
        top = self.groups * self.fsdp
        self.side_orders = [bits_of(self.fsdp) + [top], [top] + bits_of(self.fsdp)]
        self.side_masks = [subset_masks(order) for order in self.side_orders]

    def flat(self, c, j, f):
        return (c * self.ctx + j) * self.fsdp + f

    def perm(self, move):
        return [(self.flat(*dev), self.flat(*move(*dev))) for dev in self.devices]

    def chip_xor(self, masks):
        def move(c, j, f):
            i = (j * self.fsdp + f) ^ masks[c]
            return (c, i // self.fsdp, i % self.fsdp)

        return self.perm(move)

    def chip_perms(self):
        return [self.chip_xor(pair) for pair in zip(*self.chip_orders)]

    def side_perms(self):
        return [self.chip_xor(pair) for pair in zip(*self.side_orders)]

    def group_perms(self):
        return [
            self.perm(lambda c, j, f, pair=pair: (c, j ^ pair[c], f))
            for pair in zip(*self.group_orders)
        ]

    def group_direct(self, d):
        return self.perm(lambda c, j, f: (c, j ^ d, f))

    def core_swap(self):
        return self.perm(lambda c, j, f: (1 - c, j, f))

    def turn(self):
        def move(c, j, f):
            return (j // self.groups, c * self.groups + j % self.groups, f)

        return self.perm(move)

    def chunk_of(self, c, j, p):
        e, k = divmod(p, self.groups)
        return (c ^ e) * self.groups + ((j % self.groups) ^ self.group_masks[c ^ e][k])

    def outward(self, p):
        def move(c, j, f):
            return (j // self.groups, self.chunk_of(c, j, p), f)

        return self.perm(move)

    def inward(self, p):
        return [(b, a) for a, b in self.outward(p)]

    def head_block(self, c, j, p):
        e, k = divmod(p, self.groups)
        s, g = divmod(j, self.groups)
        return (s ^ e) * self.groups + (g ^ self.group_masks[s][k])

    def table(self, entries):
        return np.array([entries(*dev) for dev in self.devices], np.int32)

    def chip_gather(self):
        def entries(c, j, f):
            inverse = np.argsort(self.chip_masks[c])
            return [inverse[(j * self.fsdp + f) ^ i] for i in range(self.chips)]

        return self.table(entries)

    def chip_spread(self):
        return self.table(
            lambda c, j, f: [(j * self.fsdp + f) ^ mask for mask in self.chip_masks[c]]
        )

    def out_rows(self, rows):
        per = self.heads * HD // rows

        def entries(c, j, f):
            return [
                self.head_block(c, j, p) * per + t for p in range(self.ctx) for t in range(per)
            ]

        return self.table(entries)

    def side_pieces(self):
        def entries(c, j, f):
            return [
                (j * self.fsdp + f) ^ mask ^ (d * self.fsdp)
                for mask in self.side_masks[c]
                for d in range(self.groups)
            ]

        return self.table(entries)


def invert(table):
    return np.argsort(table, axis=1).astype(np.int32)


def route(sources, table, outs, moves):
    def kernel(table_ref, *refs):
        ins, results, sems = refs[: len(sources)], refs[len(sources) : -1], refs[-1]

        def copy(m, source, piece):
            _, _, row, rows, out, out_piece, out_row = moves[m]
            return pltpu.make_async_copy(
                source.at[piece, pl.ds(row, rows)],
                results[out].at[out_piece, pl.ds(out_row, rows)],
                sems.at[m],
            )

        for m, (group, slot, *_) in enumerate(moves):
            index = table_ref[slot]
            start = 0
            for which in group:
                count = sources[which].shape[0]

                @pl.when((index >= start) & (index < start + count))
                def _():
                    copy(m, ins[which], index - start).start()

                start += count
        for m, (group, *_) in enumerate(moves):
            copy(m, ins[group[0]], 0).wait()

    total = sum(
        moves[m][3] * outs[moves[m][4]].shape[2] * outs[moves[m][4]].dtype.itemsize
        for m in range(len(moves))
    )
    return pl.pallas_call(
        kernel,
        out_shape=outs,
        in_specs=[pl.BlockSpec(memory_space=pltpu.SMEM)]
        + [pl.BlockSpec(memory_space=pl.ANY)] * len(sources),
        out_specs=[pl.BlockSpec(memory_space=pltpu.VMEM)] * len(outs),
        scratch_shapes=[pltpu.SemaphoreType.DMA((len(moves),))],
        compiler_params=pltpu.CompilerParams(vmem_limit_bytes=VMEM_LIMIT),
        cost_estimate=pl.CostEstimate(flops=0, bytes_accessed=2 * total, transcendentals=0),
    )(table, *sources)


def nt(left, right):
    return lax.dot_general(left, right, (((1,), (1,)), ((), ())), preferred_element_type=F32)


def nn(left, right):
    return lax.dot_general(left, right, (((1,), (0,)), ((), ())), preferred_element_type=F32)


def tn(left, right):
    return lax.dot_general(left, right, (((0,), (0,)), ((), ())), preferred_element_type=F32)


def column_ids(row):
    return jnp.transpose(jnp.broadcast_to(row, (128, row.shape[1])))


def attend_forward(qkv_own, qkv_other, ids, overlap, heads):
    half, rows, width = qkv_own.shape
    chunks = 2 * half
    lanes = heads * HD

    def kernel(overlap_ref, own_ref, other_ref, ids_ref, *refs):
        outs = refs[:chunks]
        flat_ref, total_ref, keys, values, queries, cols, high, low, acc = refs[chunks:]
        step = pl.program_id(0)

        @pl.when(step == 0)
        def _():
            for p in range(chunks):
                block = (own_ref if p < half else other_ref)[p % half]
                queries[p] = block[:, :lanes] * BF(HD**-0.5)
                keys[p] = block[:, lanes : 2 * lanes]
                values[p] = jnp.transpose(block[:, 2 * lanes :])
                cols[p] = column_ids(ids_ref[p])

        high[...] = jnp.full_like(high, NEG_FILL)
        low[...] = jnp.zeros_like(low)
        acc[...] = jnp.zeros_like(acc)
        query = queries[step]
        row_ids = ids_ref[step]

        def one(p, carry):
            @pl.when(overlap_ref[step, p] > 0)
            def _():
                same = (
                    jnp.concatenate([cols[p]] * (-(-rows // 128)), axis=1)[:, :rows] == row_ids
                )
                key = keys[p]
                for h in range(heads):
                    at = slice(h * HD, (h + 1) * HD)
                    logits = jnp.where(same, nt(key[:, at], query[:, at]), NEG_FILL)
                    before = high[h : h + 1]
                    now = jnp.maximum(before, jnp.max(logits, 0, keepdims=True))
                    weights = jnp.exp(logits - now)
                    fade = jnp.exp(before - now)
                    high[h : h + 1] = now
                    low[h : h + 1] = low[h : h + 1] * fade + jnp.sum(weights, 0, keepdims=True)
                    acc[at] = acc[at] * fade + nn(values[p, at], weights.astype(BF))

            return carry

        lax.fori_loop(0, chunks, one, 0)
        flat = jnp.concatenate(
            [acc[h * HD : (h + 1) * HD] / low[h : h + 1] for h in range(heads)], axis=0
        )
        flat_ref[0] = flat
        total_ref[0] = high[...] + jnp.log(jnp.maximum(low[...], 1e-30))
        turned = jnp.transpose(flat).astype(BF)
        for p in range(chunks):

            @pl.when(step == p)
            def _():
                outs[p][...] = turned

    whole = lambda *shape: pl.BlockSpec(shape, lambda i, o: (0,) * len(shape))
    pairs = chunks * chunks * heads
    return pl.pallas_call(
        kernel,
        out_shape=[jax.ShapeDtypeStruct((rows, lanes), BF)] * chunks
        + [
            jax.ShapeDtypeStruct((chunks, lanes, rows), F32),
            jax.ShapeDtypeStruct((chunks, 8, rows), F32),
        ],
        grid_spec=pltpu.PrefetchScalarGridSpec(
            num_scalar_prefetch=1,
            grid=(chunks,),
            in_specs=[
                whole(half, rows, width),
                whole(half, rows, width),
                whole(chunks, 1, rows),
            ],
            out_specs=[whole(rows, lanes)] * chunks
            + [
                pl.BlockSpec((1, lanes, rows), lambda i, o: (i, 0, 0)),
                pl.BlockSpec((1, 8, rows), lambda i, o: (i, 0, 0)),
            ],
            scratch_shapes=[
                pltpu.VMEM((chunks, rows, lanes), BF),
                pltpu.VMEM((chunks, lanes, rows), BF),
                pltpu.VMEM((chunks, rows, lanes), BF),
                pltpu.VMEM((chunks, rows, 128), F32),
                pltpu.VMEM((8, rows), F32),
                pltpu.VMEM((8, rows), F32),
                pltpu.VMEM((lanes, rows), F32),
            ],
        ),
        compiler_params=pltpu.CompilerParams(vmem_limit_bytes=VMEM_LIMIT),
        cost_estimate=pl.CostEstimate(
            flops=pairs * rows * rows * 256,
            bytes_accessed=chunks * rows * width * 4,
            transcendentals=pairs * rows * rows,
        ),
    )(overlap, qkv_own, qkv_other, ids)


def attend_backward(qkv_own, qkv_other, ids, overlap, grads, flat, totals, heads):
    half, rows, width = qkv_own.shape
    chunks = 2 * half
    lanes = heads * HD

    def kernel(overlap_ref, own_ref, other_ref, ids_ref, flat_ref, total_ref, *refs):
        grad_refs = refs[:chunks]
        down_own, down_other = refs[chunks : chunks + 2]
        keys, turned, values, queries, ups, cols, grad_key, grad_value, acc = refs[chunks + 2 :]
        step = pl.program_id(0)

        @pl.when(step == 0)
        def _():
            for p in range(chunks):
                block = (own_ref if p < half else other_ref)[p % half]
                queries[p] = block[:, :lanes] * BF(HD**-0.5)
                keys[p] = block[:, lanes : 2 * lanes]
                turned[p] = jnp.transpose(block[:, lanes : 2 * lanes])
                values[p] = block[:, 2 * lanes :]
                ups[p] = grad_refs[p][...]
                cols[p] = column_ids(ids_ref[p])
            grad_key[...] = jnp.zeros_like(grad_key)
            grad_value[...] = jnp.zeros_like(grad_value)

        query = queries[step]
        row_ids = ids_ref[step]
        up = ups[step]
        product = jnp.transpose(up.astype(F32)) * flat_ref[0]
        deltas = [
            jnp.sum(product[h * HD : (h + 1) * HD], 0, keepdims=True) for h in range(heads)
        ]
        total = total_ref[0]
        acc[...] = jnp.zeros_like(acc)

        def one(p, carry):
            @pl.when(overlap_ref[step, p] > 0)
            def _():
                same = (
                    jnp.concatenate([cols[p]] * (-(-rows // 128)), axis=1)[:, :rows] == row_ids
                )
                key, value = keys[p], values[p]
                key_parts, value_parts = [], []
                for h in range(heads):
                    at = slice(h * HD, (h + 1) * HD)
                    logits = jnp.where(same, nt(key[:, at], query[:, at]), NEG_FILL)
                    weights = jnp.exp(logits - total[h : h + 1])
                    grad_prob = nt(value[:, at], up[:, at])
                    grad_score = (weights * (grad_prob - deltas[h])).astype(BF)
                    value_parts.append(nn(weights.astype(BF), up[:, at]))
                    key_parts.append(nn(grad_score, query[:, at]))
                    acc[at] = acc[at] + nn(turned[p, at], grad_score)
                grad_value[p] = grad_value[p] + jnp.concatenate(value_parts, axis=1)
                grad_key[p] = grad_key[p] + jnp.concatenate(key_parts, axis=1)

            return carry

        lax.fori_loop(0, chunks, one, 0)
        grad_query = (jnp.transpose(acc[...]) * HD**-0.5).astype(BF)
        for p in range(chunks):
            out = down_own if p < half else down_other

            @pl.when(step == p)
            def _():
                out[p % half, :, :lanes] = grad_query

            @pl.when(step == chunks - 1)
            def _():
                out[p % half, :, lanes : 2 * lanes] = grad_key[p].astype(BF)
                out[p % half, :, 2 * lanes :] = grad_value[p].astype(BF)

    whole = lambda *shape: pl.BlockSpec(shape, lambda i, o: (0,) * len(shape))
    pairs = chunks * chunks * heads
    return pl.pallas_call(
        kernel,
        out_shape=[jax.ShapeDtypeStruct((half, rows, width), BF)] * 2,
        grid_spec=pltpu.PrefetchScalarGridSpec(
            num_scalar_prefetch=1,
            grid=(chunks,),
            in_specs=[
                whole(half, rows, width),
                whole(half, rows, width),
                whole(chunks, 1, rows),
                pl.BlockSpec((1, lanes, rows), lambda i, o: (i, 0, 0)),
                pl.BlockSpec((1, 8, rows), lambda i, o: (i, 0, 0)),
            ]
            + [whole(rows, lanes)] * chunks,
            out_specs=[whole(half, rows, width)] * 2,
            scratch_shapes=[
                pltpu.VMEM((chunks, rows, lanes), BF),
                pltpu.VMEM((chunks, lanes, rows), BF),
                pltpu.VMEM((chunks, rows, lanes), BF),
                pltpu.VMEM((chunks, rows, lanes), BF),
                pltpu.VMEM((chunks, rows, lanes), BF),
                pltpu.VMEM((chunks, rows, 128), F32),
                pltpu.VMEM((chunks, rows, lanes), F32),
                pltpu.VMEM((chunks, rows, lanes), F32),
                pltpu.VMEM((lanes, rows), F32),
            ],
        ),
        compiler_params=pltpu.CompilerParams(vmem_limit_bytes=VMEM_LIMIT),
        cost_estimate=pl.CostEstimate(
            flops=pairs * rows * rows * 640,
            bytes_accessed=chunks * rows * width * 8,
            transcendentals=pairs * rows * rows,
        ),
    )(overlap, qkv_own, qkv_other, ids, flat, totals, *grads)


def layer_norm_forward(hidden, norm_gain, norm_shift):
    centered_input = hidden - jnp.mean(hidden, -1, keepdims=True)
    inverse_deviation = lax.rsqrt(
        jnp.mean(centered_input * centered_input, -1, keepdims=True) + NORM_EPS
    )
    standardized_input = centered_input * inverse_deviation
    return (standardized_input * norm_gain + norm_shift, standardized_input, inverse_deviation)


def layer_norm_backward(upstream_gradient, standardized_input, inverse_deviation, norm_gain):
    scaled_rows = upstream_gradient * norm_gain
    centered_input = (
        scaled_rows
        - jnp.mean(scaled_rows, -1, keepdims=True)
        - standardized_input * jnp.mean(scaled_rows * standardized_input, -1, keepdims=True)
    )
    return (
        inverse_deviation * centered_input,
        jnp.sum(upstream_gradient * standardized_input, 0),
        jnp.sum(upstream_gradient, 0),
    )


def send(value, perm):
    return lax.ppermute(value, AXES, perm)


def gather_stages(block, perms):
    for perm in perms[:-1]:
        block = jnp.concatenate([block, send(block, perm)], axis=0)
    return [block, send(block, perms[-1])]


def scatter_stages(keep, away, perms):
    for perm in perms[:0:-1]:
        arrived = send(away, perm).astype(F32)
        half = keep.shape[0] // 2
        keep = keep.astype(F32)
        away = (keep[half:] + arrived[half:]).astype(BF)
        keep = keep[:half] + arrived[:half]
        keep = keep.astype(BF)
    return keep.astype(F32) + send(away, perms[0]).astype(F32)


def pieces(count, rows, columns):
    return jax.ShapeDtypeStruct((count, rows, columns), BF)


def body(
    plan,
    tokens,
    segment_ids,
    w_query,
    b_query,
    w_key,
    w_value,
    b_value,
    w_out,
    b_out,
    g_attn,
    n_attn,
    w_in,
    b_in,
    w_back,
    b_back,
    g_ffn,
    n_ffn,
    cotangent,
):
    chips, groups, heads, ctx = plan.chips, plan.groups, plan.heads, plan.ctx
    core = lax.axis_index("dp")
    place = lax.axis_index("ctx")
    device = (core * ctx + place) * plan.fsdp + lax.axis_index("fsdp")
    side, group = place // groups, place % groups
    rows = tokens.shape[1]
    shard = w_query.shape[0]
    hidden = w_back.shape[0]
    part = hidden // 2
    lanes = heads * HD
    half_d = D // 2
    width = 3 * lanes
    vectors = (b_query, b_value, b_out, g_attn, n_attn, b_back, g_ffn, n_ffn)
    extra_size = len(vectors) * shard + hidden + rows
    extra_rows = 16 * (-(-extra_size // (16 * width)))
    swap = plan.core_swap()

    def lookup(table):
        return lax.dynamic_index_in_dim(jnp.asarray(table), device, 0, False)

    def mine(columns, size, axis=1):
        return lax.dynamic_slice_in_dim(columns, core * size, size, axis)

    inputs = tokens[0]
    block = send(inputs, plan.turn())[None]
    for perm in plan.group_perms():
        block = jnp.concatenate([block, send(block, perm)], axis=0)
    tokens_own = block
    tokens_other = send(tokens_own, swap)

    extra = jnp.concatenate(list(vectors) + [b_in, segment_ids[0].astype(BF)])
    extra = jnp.pad(extra, (0, extra_rows * width - extra_size)).reshape(extra_rows, width)
    heads_in = jnp.stack(
        [mine(w, half_d).reshape(shard, groups, lanes) for w in (w_query, w_key, w_value)], axis=2
    ).reshape(shard, groups, width)

    def message(d):
        columns = lax.dynamic_index_in_dim(heads_in, group ^ d, 1, False)
        return jnp.concatenate([columns, extra], axis=0)

    arrived = [message(0)] + [
        send(message(d), plan.group_direct(d)) for d in range(1, groups)
    ]
    gathered = gather_stages(jnp.stack(arrived), plan.side_perms())
    side_table = plan.side_pieces()
    heads_mat, extras = route(
        gathered,
        lookup(invert(side_table)),
        [pieces(chips, shard, width), pieces(chips, extra_rows, width)],
        [((0, 1), i, 0, shard, 0, i, 0) for i in range(chips)]
        + [((0, 1), i, shard, extra_rows, 1, i, 0) for i in range(chips)],
    )
    heads_mat = heads_mat.reshape(D, width)
    extras = extras.reshape(chips, -1)

    def vector(which):
        return extras[:, which * shard : (which + 1) * shard].reshape(-1)

    query_bias, value_bias, out_bias, gain_one, shift_one, back_bias, gain_two, shift_two = [
        vector(which) for which in range(len(vectors))
    ]
    at = len(vectors) * shard
    in_bias = lax.dynamic_index_in_dim(
        extras[:, at : at + hidden].reshape(chips, 2, part), core, 1, False
    ).reshape(-1)
    ids_here = lax.dynamic_index_in_dim(
        extras[:, at + hidden : at + hidden + rows].reshape(ctx, plan.fsdp, rows),
        lax.axis_index("fsdp"),
        1,
        False,
    )
    ids_there = send(ids_here, swap)
    ids_all = jnp.where(core == side, ids_here, ids_there).astype(F32)
    chunk_table = plan.table(lambda c, j, f: [plan.chunk_of(c, j, p) for p in range(ctx)])
    chosen = lookup(chunk_table)[:, None] == jnp.arange(ctx)[None]
    ids = jnp.sum(jnp.where(chosen[:, :, None], ids_all[None], 0.0), axis=1)
    first, last = ids[:, 0], ids[:, -1]
    overlap = ((first[:, None] <= last[None]) & (first[None] <= last[:, None])).astype(jnp.int32)
    ids = ids[:, None, :]

    perms = plan.chip_perms()
    out_parts = gather_stages(mine(w_out, half_d)[None], perms)
    w_in_mine = lax.dynamic_index_in_dim(
        w_in.reshape(shard, chips, 2, part), core, 2, False
    ).reshape(shard, chips * part)
    in_parts = gather_stages(w_in_mine[None], perms)
    back_parts = gather_stages(mine(w_back, part, 0)[None], perms)
    chip_gather = plan.chip_gather()
    out_table = plan.out_rows(shard)
    out_gather = np.take_along_axis(chip_gather, out_table, axis=1)

    def placed(parts, table):
        _, piece_rows, columns = parts[0].shape
        (result,) = route(
            parts,
            lookup(table),
            [pieces(chips, piece_rows, columns)],
            [((0, 1), i, 0, piece_rows, 0, i, 0) for i in range(chips)],
        )
        return result.reshape(chips * piece_rows, columns)

    out_mine = placed(out_parts, out_gather)
    out_there = send(out_mine, swap)
    out_mat = jnp.where(
        core == 0,
        jnp.concatenate([out_mine, out_there], axis=1),
        jnp.concatenate([out_there, out_mine], axis=1),
    )
    in_mat = placed(in_parts, chip_gather)
    back_mat = placed(back_parts, chip_gather)

    start = core * half_d + group * lanes
    zero_bias = jnp.zeros((lanes,), BF)
    heads_bias = jnp.concatenate(
        [
            lax.dynamic_slice_in_dim(query_bias, start, lanes),
            zero_bias,
            lax.dynamic_slice_in_dim(value_bias, start, lanes),
        ]
    ).astype(F32)

    def project(block):
        return (
            jnp.einsum("ptd,dw->ptw", block, heads_mat, preferred_element_type=F32) + heads_bias
        ).astype(BF)

    qkv_own, qkv_other = project(tokens_own), project(tokens_other)
    *sent, flat, totals = attend_forward(qkv_own, qkv_other, ids, overlap, heads)
    attended = jnp.concatenate([send(sent[p], plan.outward(p)) for p in range(ctx)], axis=1)

    branch = nn(attended, out_mat) + out_bias
    normed, standard_one, inverse_one = layer_norm_forward(
        inputs.astype(F32) + branch, gain_one, shift_one
    )
    low_own = normed.astype(BF)
    low_other = send(low_own, swap)

    def feed(low):
        inner = nn(low, in_mat) + in_bias
        cdf = 0.5 * (1.0 + lax.erf(inner * (0.5**0.5)))
        slope = cdf + inner * (jnp.exp(-0.5 * inner * inner) * (1.0 / (2.0 * np.pi) ** 0.5))
        return (inner * cdf).astype(BF), slope

    active_own, slope_own = feed(low_own)
    active_other, slope_other = feed(low_other)
    fed = nn(active_own, back_mat) + send(nn(active_other, back_mat), swap) + back_bias
    result, standard_two, inverse_two = layer_norm_forward(normed + fed, gain_two, shift_two)
    grad_sum_two, grad_gain_two, grad_shift_two = layer_norm_backward(
        cotangent[0].astype(F32), standard_two, inverse_two, gain_two
    )
    up_own = grad_sum_two.astype(BF)
    up_other = send(up_own, swap)
    grad_back_bias = jnp.sum(up_own.astype(F32), 0)

    grad_inner_own = (nt(up_own, back_mat) * slope_own).astype(BF)
    grad_inner_other = (nt(up_other, back_mat) * slope_other).astype(BF)
    chip_spread = plan.chip_spread()

    def spread(grad, table, piece_rows):
        columns = grad.shape[1]
        keep, away = route(
            [grad.astype(BF).reshape(chips, piece_rows, columns)],
            lookup(table),
            [pieces(chips // 2, piece_rows, columns)] * 2,
            [
                ((0,), k, 0, piece_rows, k // (chips // 2), k % (chips // 2), 0)
                for k in range(chips)
            ],
        )
        return scatter_stages(keep, away, perms)[0]

    grad_back_mat = spread(
        tn(active_own, up_own) + tn(active_other, up_other), chip_spread, part
    )
    grad_in_mat = spread(
        tn(low_own, grad_inner_own) + tn(low_other, grad_inner_other), chip_spread, shard
    )
    grad_in_bias = jnp.sum(grad_inner_own.astype(F32), 0) + jnp.sum(
        grad_inner_other.astype(F32), 0
    )
    grad_normed = (
        grad_sum_two + nt(grad_inner_own, in_mat) + send(nt(grad_inner_other, in_mat), swap)
    )
    grad_sum_one, grad_gain_one, grad_shift_one = layer_norm_backward(
        grad_normed, standard_one, inverse_one, gain_one
    )
    grad_branch = grad_sum_one.astype(BF)
    grad_out_bias = jnp.sum(grad_branch.astype(F32), 0)
    grad_attended = nt(grad_branch, out_mat).astype(BF)
    grads = [
        send(grad_attended[:, p * lanes : (p + 1) * lanes], plan.inward(p)) for p in range(ctx)
    ]
    grad_out_mine = tn(attended, mine(grad_branch, half_d))
    grad_out_there = tn(
        attended, lax.dynamic_slice_in_dim(grad_branch, (1 - core) * half_d, half_d, 1)
    )
    grad_out = grad_out_mine + send(grad_out_there.astype(BF), swap).astype(F32)
    out_spread = np.take_along_axis(invert(out_table), chip_spread, axis=1)
    grad_out_mat = spread(grad_out, out_spread, shard)

    down_own, down_other = attend_backward(
        qkv_own, qkv_other, ids, overlap, grads, flat, totals, heads
    )

    def back_project(down):
        return jnp.einsum("ptw,dw->ptd", down, heads_mat, preferred_element_type=F32)

    towards = send(back_project(down_other).astype(BF), swap)
    block = (back_project(down_own) + towards.astype(F32)).astype(BF)
    for perm in plan.group_perms()[::-1]:
        half = block.shape[0] // 2
        block = (block[:half].astype(F32) + send(block[half:], perm).astype(F32)).astype(BF)
    grad_inputs = grad_sum_one + send(block[0], plan.turn()).astype(F32)

    grad_heads = jnp.einsum(
        "ptd,ptw->dw", tokens_own, down_own, preferred_element_type=F32
    ) + jnp.einsum("ptd,ptw->dw", tokens_other, down_other, preferred_element_type=F32)
    grad_heads_bias = jnp.sum(down_own.astype(F32), (0, 1)) + jnp.sum(
        down_other.astype(F32), (0, 1)
    )

    def whole_bias(columns):
        return lax.dynamic_update_slice_in_dim(jnp.zeros((D,), F32), columns, start, 0)

    grad_vectors = (
        whole_bias(grad_heads_bias[:lanes]),
        whole_bias(grad_heads_bias[2 * lanes :]),
        grad_out_bias,
        grad_gain_one,
        grad_shift_one,
        grad_back_bias,
        grad_gain_two,
        grad_shift_two,
    )
    in_pairs = grad_in_bias.reshape(chips, 1, part) * (
        jnp.arange(2)[None, :, None] == core
    ).astype(F32)
    grad_extra = jnp.concatenate(
        [grad.reshape(chips, shard) for grad in grad_vectors]
        + [in_pairs.reshape(chips, hidden)],
        axis=1,
    )
    grad_extra = jnp.pad(
        grad_extra, ((0, 0), (0, extra_rows * width - grad_extra.shape[1]))
    ).reshape(chips, extra_rows, width)
    keep, away = route(
        [grad_heads.astype(BF).reshape(chips, shard, width), grad_extra.astype(BF)],
        lookup(side_table),
        [pieces(chips // 2, shard + extra_rows, width)] * 2,
        [
            ((which,), k, 0, size, k // (chips // 2), k % (chips // 2), which * shard)
            for which, size in ((0, shard), (1, extra_rows))
            for k in range(chips)
        ],
    )
    mine_by_group = scatter_stages(keep, away, plan.side_perms())
    low_by_group = mine_by_group.astype(BF)
    by_group = [low_by_group[0]] + [
        send(low_by_group[d], plan.group_direct(d)) for d in range(1, groups)
    ]
    by_group = jnp.stack(by_group).astype(F32)
    grad_extras = jnp.sum(by_group[:, shard:], 0)
    grad_columns = jnp.stack(
        [lax.dynamic_index_in_dim(by_group, group ^ d, 0, False)[:shard] for d in range(groups)]
    )
    grad_columns = grad_columns.reshape(groups, shard, 3, lanes).transpose(2, 1, 0, 3)
    grad_columns = grad_columns.reshape(3, shard, half_d)

    def both(half, axis):
        there = send(half, swap)
        return jnp.where(
            core == 0, jnp.stack([half, there], axis=axis), jnp.stack([there, half], axis=axis)
        )

    grad_columns = both(grad_columns, 2).reshape(3, shard, D)
    grad_out_mat = both(grad_out_mat, 1).reshape(shard, D)
    grad_in_mat = both(grad_in_mat.reshape(shard, chips, part), 2).reshape(shard, FF)
    grad_back_mat = both(grad_back_mat, 0).reshape(hidden, D)
    sums = (grad_extras + send(grad_extras, swap)).reshape(-1)
    small = [sums[which * shard : (which + 1) * shard] for which in range(len(vectors))]
    return (
        result.astype(BF)[None],
        grad_inputs[None],
        grad_columns[0],
        small[0],
        grad_columns[1],
        grad_columns[2],
        small[1],
        grad_out_mat,
        small[2],
        small[3],
        small[4],
        grad_in_mat,
        sums[at : at + hidden],
        grad_back_mat,
        small[5],
        small[6],
        small[7],
    )


def solution(mesh):
    owned = ("ctx", "fsdp")
    matrix, vector = P(owned, None), P(owned)
    sequence = P(("dp", "fsdp"), "ctx", None)
    return jax.shard_map(
        partial(body, Plan(mesh)),
        mesh=mesh,
        in_specs=(
            sequence,
            P(("dp", "fsdp"), "ctx"),
            matrix,
            vector,
            matrix,
            matrix,
            vector,
            matrix,
            vector,
            vector,
            vector,
            matrix,
            vector,
            matrix,
            vector,
            vector,
            vector,
            sequence,
        ),
        out_specs=(
            sequence,
            sequence,
            matrix,
            vector,
            matrix,
            matrix,
            vector,
            matrix,
            vector,
            vector,
            vector,
            matrix,
            vector,
            matrix,
            vector,
            vector,
            vector,
        ),
        check_vma=False,
    )
```

```python
from functools import partial

import jax
import jax.numpy as jnp
import numpy as np
from jax import lax
from jax.experimental import pallas as pl
from jax.experimental.pallas import tpu as pltpu
from jax.sharding import PartitionSpec as P

D = 1024
H = 16
HD = 64
FF = 4096
NORM_EPS = 1e-05
NEG_FILL = -1e30
AXES = ("dp", "ctx", "fsdp")
BF = jnp.bfloat16
F32 = jnp.float32
VMEM_LIMIT = 48 * 1024 * 1024


def subset_masks(order):
    table = [0]
    for mask in order:
        table = table + [mask ^ entry for entry in table]
    return table


def bits_of(count):
    return [1 << t for t in range(count.bit_length() - 1)]


class Plan:
    def __init__(self, mesh):
        self.ctx = mesh.shape["ctx"]
        self.fsdp = mesh.shape["fsdp"]
        self.chips = self.ctx * self.fsdp
        self.groups = self.ctx // 2
        self.heads = H // self.ctx
        self.devices = [
            (c, j, f) for c in range(2) for j in range(self.ctx) for f in range(self.fsdp)
        ]
        bits = bits_of(self.chips)
        self.in_orders = [bits[:1:-1] + [1, 2], bits[:1:-1] + [2, 1]]
        self.back_orders = self.in_orders
        group_bits = bits_of(self.groups)
        self.group_orders = [group_bits[::-1], group_bits]
        self.group_masks = [subset_masks(order) for order in self.group_orders]
        top = self.groups * self.fsdp
        self.side_orders = [[top] + bits_of(self.fsdp)] * 2
        self.side_masks = [subset_masks(order) for order in self.side_orders]

    def flat(self, c, j, f):
        return (c * self.ctx + j) * self.fsdp + f

    def perm(self, move):
        return [(self.flat(*dev), self.flat(*move(*dev))) for dev in self.devices]

    def chip_xor(self, masks):
        def move(c, j, f):
            i = (j * self.fsdp + f) ^ masks[c]
            return (c, i // self.fsdp, i % self.fsdp)

        return self.perm(move)

    def chip_perms(self, orders):
        return [self.chip_xor(pair) for pair in zip(*orders)]

    def side_perms(self):
        return [self.chip_xor(pair) for pair in zip(*self.side_orders)]

    def group_perms(self):
        return [
            self.perm(lambda c, j, f, pair=pair: (c, j ^ pair[c], f))
            for pair in zip(*self.group_orders)
        ]

    def group_direct(self, d):
        return self.perm(lambda c, j, f: (c, j ^ d, f))

    def core_swap(self):
        return self.perm(lambda c, j, f: (1 - c, j, f))

    def turn(self):
        def move(c, j, f):
            return (j // self.groups, c * self.groups + j % self.groups, f)

        return self.perm(move)

    def chunk_of(self, c, j, p):
        e, k = divmod(p, self.groups)
        return (c ^ e) * self.groups + ((j % self.groups) ^ self.group_masks[c ^ e][k])

    def table(self, entries):
        return np.array([entries(*dev) for dev in self.devices], np.int32)

    def chip_gather(self, orders):
        def entries(c, j, f):
            inverse = np.argsort(subset_masks(orders[c]))
            return [inverse[(j * self.fsdp + f) ^ i] for i in range(self.chips)]

        return self.table(entries)

    def side_pieces(self):
        def entries(c, j, f):
            return [
                (j * self.fsdp + f) ^ mask ^ (d * self.fsdp)
                for mask in self.side_masks[c]
                for d in range(self.groups)
            ]

        return self.table(entries)


def invert(table):
    return np.argsort(table, axis=1).astype(np.int32)


def route(sources, table, outs, moves):
    def kernel(table_ref, *refs):
        ins, results, sems = refs[: len(sources)], refs[len(sources) : -1], refs[-1]

        def copy(m, source, piece):
            _, _, row, rows, out, out_piece, out_row = moves[m]
            return pltpu.make_async_copy(
                source.at[piece, pl.ds(row, rows)],
                results[out].at[out_piece, pl.ds(out_row, rows)],
                sems.at[m],
            )

        for m, (group, slot, *_) in enumerate(moves):
            index = table_ref[slot]
            start = 0
            for which in group:
                count = sources[which].shape[0]

                @pl.when((index >= start) & (index < start + count))
                def _():
                    copy(m, ins[which], index - start).start()

                start += count
        for m, (group, *_) in enumerate(moves):
            copy(m, ins[group[0]], 0).wait()

    total = sum(
        moves[m][3] * outs[moves[m][4]].shape[2] * outs[moves[m][4]].dtype.itemsize
        for m in range(len(moves))
    )
    return pl.pallas_call(
        kernel,
        out_shape=outs,
        in_specs=[pl.BlockSpec(memory_space=pltpu.SMEM)]
        + [pl.BlockSpec(memory_space=pl.ANY)] * len(sources),
        out_specs=[pl.BlockSpec(memory_space=pltpu.VMEM)] * len(outs),
        scratch_shapes=[pltpu.SemaphoreType.DMA((len(moves),))],
        compiler_params=pltpu.CompilerParams(vmem_limit_bytes=VMEM_LIMIT),
        cost_estimate=pl.CostEstimate(flops=0, bytes_accessed=0, transcendentals=0),
    )(table, *sources)


def nt(left, right):
    return lax.dot_general(left, right, (((1,), (1,)), ((), ())), preferred_element_type=F32)


def nn(left, right):
    return lax.dot_general(left, right, (((1,), (0,)), ((), ())), preferred_element_type=F32)


def tn(left, right):
    return lax.dot_general(left, right, (((0,), (0,)), ((), ())), preferred_element_type=F32)


def column_ids(row):
    return jnp.transpose(jnp.broadcast_to(row, (128, row.shape[1])))


def listing(overlap):
    count = overlap.shape[0]
    before = jnp.arange(count)[None, :] < jnp.arange(count)[:, None]
    rank = jnp.sum(jnp.where(before[None], overlap[:, None, :], 0), 2)
    slot = jnp.where(overlap > 0, rank, count)
    here = slot[:, None, :] == jnp.arange(count)[None, :, None]
    order = jnp.sum(jnp.where(here, jnp.arange(count)[None, None, :], 0), 2)
    return jnp.concatenate([order, jnp.sum(overlap, 1, keepdims=True)], 1).astype(jnp.int32)


def fold(values, combine):
    rows = values.shape[0]
    while rows > 8:
        rows //= 2
        values = combine(values[:rows], values[rows:])
    return values


def looped(count, step, carry):
    pairs = count // 2
    carry = lax.fori_loop(0, pairs, lambda t, c: step(2 * t + 1, step(2 * t, c)), carry)
    return lax.fori_loop(2 * pairs, count, step, carry)


def same_document(columns, row):
    repeats = -(-columns.shape[0] // 128)
    return jnp.concatenate([columns] * repeats, axis=1)[:, : row.shape[1]] == row


def one_head(flat, h, heads):
    zero = jnp.zeros((HD, flat.shape[1]), flat.dtype)
    return jnp.concatenate(
        [flat[g * HD : (g + 1) * HD] if g == h else zero for g in range(heads)], axis=0
    )


def attend_forward(places, qkv_own, qkv_other, ids, meets, heads):
    half, rows, width = qkv_own.shape
    chunks = 2 * half
    lanes = heads * HD

    def kernel(list_ref, place_ref, own_ref, other_ref, ids_ref, *refs):
        out_ref, flat_ref, total_ref, keys, values, queries, cols, logits_ref = refs
        step = pl.program_id(0)

        @pl.when(step == 0)
        def _():
            for p in range(chunks):
                block = (own_ref if p < half else other_ref)[p % half]
                query = jnp.transpose(block[:, :lanes] * BF(HD**-0.5))
                for h in range(heads):
                    queries[p, h] = one_head(query, h, heads)
                keys[p] = block[:, lanes : 2 * lanes]
                values[p] = jnp.transpose(block[:, 2 * lanes :])
                cols[p] = column_ids(ids_ref[p])

        row_ids = ids_ref[step]
        count = list_ref[step, chunks]
        query = [queries[step, h] for h in range(heads)]

        def scores(t, highs):
            p = list_ref[step, t]
            same = same_document(cols[p], row_ids)
            key = keys[p]
            new = []
            for h in range(heads):
                logits = jnp.where(same, nn(key, query[h]), NEG_FILL)
                logits_ref[h, t] = logits
                new.append(jnp.maximum(highs[h], fold(logits, jnp.maximum)))
            return tuple(new)

        highs = looped(
            count, scores, tuple(jnp.full((8, rows), NEG_FILL, F32) for _ in range(heads))
        )
        highs = [jnp.max(high, 0, keepdims=True) for high in highs]

        def attend(t, sums):
            p = list_ref[step, t]
            new = []
            for h in range(heads):
                low, acc = sums[h]
                weights = jnp.exp(logits_ref[h, t] - highs[h])
                new.append(
                    (
                        low + fold(weights, jnp.add),
                        acc + nn(values[p, h * HD : (h + 1) * HD], weights.astype(BF)),
                    )
                )
            return tuple(new)

        sums = looped(
            count,
            attend,
            tuple(
                (jnp.zeros((8, rows), F32), jnp.zeros((HD, rows), F32)) for _ in range(heads)
            ),
        )
        lows = [jnp.sum(low, 0, keepdims=True) for low, _ in sums]
        flat = jnp.concatenate([acc / low for (_, acc), low in zip(sums, lows)], axis=0)
        flat_ref[0] = flat
        total_ref[0] = jnp.concatenate(
            [high + jnp.log(low) for high, low in zip(highs, lows)]
            + [jnp.zeros((8 - heads, rows), F32)],
            axis=0,
        )
        out_ref[0] = jnp.transpose(flat).astype(BF)

    whole = lambda *shape: pl.BlockSpec(shape, lambda i, o, q: (0,) * len(shape))
    pairs = chunks * chunks * heads
    return pl.pallas_call(
        kernel,
        name="attend_forward",
        out_shape=[
            jax.ShapeDtypeStruct((chunks, rows, lanes), BF),
            jax.ShapeDtypeStruct((chunks, lanes, rows), F32),
            jax.ShapeDtypeStruct((chunks, 8, rows), F32),
        ],
        grid_spec=pltpu.PrefetchScalarGridSpec(
            num_scalar_prefetch=2,
            grid=(chunks,),
            in_specs=[
                whole(half, rows, width),
                whole(half, rows, width),
                whole(chunks, 1, rows),
            ],
            out_specs=[
                pl.BlockSpec((1, rows, lanes), lambda i, o, q: (q[i], 0, 0)),
                pl.BlockSpec((1, lanes, rows), lambda i, o, q: (i, 0, 0)),
                pl.BlockSpec((1, 8, rows), lambda i, o, q: (i, 0, 0)),
            ],
            scratch_shapes=[
                pltpu.VMEM((chunks, rows, lanes), BF),
                pltpu.VMEM((chunks, lanes, rows), BF),
                pltpu.VMEM((chunks, heads, lanes, rows), BF),
                pltpu.VMEM((chunks, rows, 128), F32),
                pltpu.VMEM((heads, chunks, rows, rows), F32),
            ],
        ),
        compiler_params=pltpu.CompilerParams(vmem_limit_bytes=VMEM_LIMIT),
        cost_estimate=pl.CostEstimate(
            flops=pairs * rows * rows * 24000,
            bytes_accessed=chunks * rows * width * 4,
            transcendentals=pairs * rows * rows,
        ),
    )(meets, places, qkv_own, qkv_other, ids)


def attend_backward(places, qkv_own, qkv_other, ids, meets, grads, flat, totals, heads):
    half, rows, width = qkv_own.shape
    chunks = 2 * half
    lanes = heads * HD

    def kernel(
        list_ref, place_ref, own_ref, other_ref, ids_ref, flat_ref, total_ref, up_ref, *refs
    ):
        down_own, down_other = refs[:2]
        keys, turned, values, queries, cols, grad_key, grad_value = refs[2:]
        step = pl.program_id(0)

        @pl.when(step == 0)
        def _():
            for p in range(chunks):
                block = (own_ref if p < half else other_ref)[p % half]
                queries[p] = block[:, :lanes] * BF(HD**-0.5)
                keys[p] = block[:, lanes : 2 * lanes]
                turned[p] = jnp.transpose(block[:, lanes : 2 * lanes])
                values[p] = block[:, 2 * lanes :]
                cols[p] = column_ids(ids_ref[p])
            grad_key[...] = jnp.zeros_like(grad_key)
            grad_value[...] = jnp.zeros_like(grad_value)

        query = queries[step]
        up = up_ref[0]
        row_ids = ids_ref[step]
        count = list_ref[step, chunks]
        query_turned, up_turned = jnp.transpose(query), jnp.transpose(up)
        product = up_turned.astype(F32) * flat_ref[0]
        deltas = [
            jnp.sum(product[h * HD : (h + 1) * HD], 0, keepdims=True) for h in range(heads)
        ]
        total = total_ref[0]
        lane_head = lax.broadcasted_iota(jnp.int32, (rows, lanes), 1) // HD
        queries_turned = [one_head(query_turned, h, heads) for h in range(heads)]
        ups_turned = [one_head(up_turned, h, heads) for h in range(heads)]
        queries_wide = [jnp.where(lane_head == h, query, BF(0)) for h in range(heads)]
        ups_wide = [jnp.where(lane_head == h, up, BF(0)) for h in range(heads)]

        def one(t, carry):
            p = list_ref[step, t]
            same = same_document(cols[p], row_ids)
            key, value = keys[p], values[p]
            sum_key, sum_value = grad_key[p], grad_value[p]
            new = []
            for h in range(heads):
                logits = jnp.where(same, nn(key, queries_turned[h]), NEG_FILL)
                weights = jnp.exp(logits - total[h : h + 1])
                grad_prob = nn(value, ups_turned[h])
                grad_score = (weights * (grad_prob - deltas[h])).astype(BF)
                sum_value = sum_value + nn(weights.astype(BF), ups_wide[h])
                sum_key = sum_key + nn(grad_score, queries_wide[h])
                new.append(carry[h] + nn(turned[p, h * HD : (h + 1) * HD], grad_score))
            grad_value[p] = sum_value
            grad_key[p] = sum_key
            return tuple(new)

        acc = looped(count, one, tuple(jnp.zeros((HD, rows), F32) for _ in range(heads)))
        grad_query = (jnp.transpose(jnp.concatenate(acc, 0)) * HD**-0.5).astype(BF)
        for p in range(chunks):
            out = down_own if p < half else down_other

            @pl.when(step == p)
            def _():
                out[p % half, :, :lanes] = grad_query

            @pl.when(step == chunks - 1)
            def _():
                out[p % half, :, lanes : 2 * lanes] = grad_key[p].astype(BF)
                out[p % half, :, 2 * lanes :] = grad_value[p].astype(BF)

    whole = lambda *shape: pl.BlockSpec(shape, lambda i, o, q: (0,) * len(shape))
    pairs = chunks * chunks * heads
    return pl.pallas_call(
        kernel,
        name="attend_backward",
        out_shape=[jax.ShapeDtypeStruct((half, rows, width), BF)] * 2,
        grid_spec=pltpu.PrefetchScalarGridSpec(
            num_scalar_prefetch=2,
            grid=(chunks,),
            in_specs=[
                whole(half, rows, width),
                whole(half, rows, width),
                whole(chunks, 1, rows),
                pl.BlockSpec((1, lanes, rows), lambda i, o, q: (i, 0, 0)),
                pl.BlockSpec((1, 8, rows), lambda i, o, q: (i, 0, 0)),
                pl.BlockSpec((1, rows, lanes), lambda i, o, q: (q[i], 0, 0)),
            ],
            out_specs=[whole(half, rows, width)] * 2,
            scratch_shapes=[
                pltpu.VMEM((chunks, rows, lanes), BF),
                pltpu.VMEM((chunks, lanes, rows), BF),
                pltpu.VMEM((chunks, rows, lanes), BF),
                pltpu.VMEM((chunks, rows, lanes), BF),
                pltpu.VMEM((chunks, rows, 128), F32),
                pltpu.VMEM((chunks, rows, lanes), F32),
                pltpu.VMEM((chunks, rows, lanes), F32),
            ],
        ),
        compiler_params=pltpu.CompilerParams(vmem_limit_bytes=VMEM_LIMIT),
        cost_estimate=pl.CostEstimate(
            flops=pairs * rows * rows * 24000,
            bytes_accessed=chunks * rows * width * 8,
            transcendentals=pairs * rows * rows,
        ),
    )(meets, places, qkv_own, qkv_other, ids, flat, totals, grads)


def block_call(kernel, name, outs, tables, blocks, hbm, scratch, flops):
    moved = sum(x.size * x.dtype.itemsize for x in (*blocks, *hbm, *outs))
    return pl.pallas_call(
        kernel,
        name=name,
        out_shape=list(outs),
        in_specs=[pl.BlockSpec(memory_space=pltpu.SMEM)] * len(tables)
        + [pl.BlockSpec(memory_space=pltpu.VMEM)] * len(blocks)
        + [pl.BlockSpec(memory_space=pl.ANY)] * len(hbm),
        out_specs=[pl.BlockSpec(memory_space=pltpu.VMEM)] * len(outs),
        scratch_shapes=list(scratch),
        compiler_params=pltpu.CompilerParams(vmem_limit_bytes=VMEM_LIMIT),
        cost_estimate=pl.CostEstimate(flops=0, bytes_accessed=0, transcendentals=0),
    )(*tables, *blocks, *hbm)


def shaped(shape, dtype=BF):
    return jax.ShapeDtypeStruct(shape, dtype)


class Fetch:
    def __init__(self, table_ref, parts, columns, target, sems, at=0):
        self.table, self.parts, self.sems = table_ref, parts, sems
        self.source = pl.ds(*columns)
        self.target, self.place = target, pl.ds(at, columns[1])
        self.rows = parts[0].shape[1]
        self.count = target.shape[0] // self.rows

    def copy(self, part, piece, i):
        rows = pl.ds(pl.multiple_of(i * self.rows, self.rows), self.rows)
        return pltpu.make_async_copy(
            part.at[piece, :, self.source], self.target.at[rows, self.place], self.sems.at[i]
        )

    def start(self):
        def one(i, carry):
            index = self.table[i]
            first = 0
            for part in self.parts:
                count = part.shape[0]

                @pl.when((index >= first) & (index < first + count))
                def _():
                    self.copy(part, index - first, i).start()

                first += count
            return carry

        lax.fori_loop(0, self.count, one, 0)

    def wait(self):
        def one(i, carry):
            self.copy(self.parts[0], 0, i).wait()
            return carry

        lax.fori_loop(0, self.count, one, 0)


def row_blocks(rows, size=32):
    return [slice(r, r + size) for r in range(0, rows, size)]


def standardize(hidden):
    centered_input = hidden - jnp.mean(hidden, -1, keepdims=True)
    inverse_deviation = lax.rsqrt(
        jnp.mean(centered_input * centered_input, -1, keepdims=True) + NORM_EPS
    )
    return centered_input * inverse_deviation, inverse_deviation


def norm_backward(upstream_gradient, standardized_input, inverse_deviation, norm_gain):
    scaled_rows = upstream_gradient * norm_gain
    return inverse_deviation * (
        scaled_rows
        - jnp.mean(scaled_rows, -1, keepdims=True)
        - standardized_input * jnp.mean(scaled_rows * standardized_input, -1, keepdims=True)
    )


def out_norm(core, here, there, inputs, vectors, matrix):
    groups, rows, lanes = here.shape
    half = D // 2

    def kernel(
        core_ref,
        here_ref,
        there_ref,
        input_ref,
        vector_ref,
        matrix_ref,
        normed,
        standard,
        inverse,
        low,
        attended,
        branch,
    ):
        for c in range(2):

            @pl.when(core_ref[0] == c)
            def _():
                for g in range(groups):
                    at = slice(c * half + g * lanes, c * half + (g + 1) * lanes)
                    attended[:, at] = here_ref[g]
                    at = slice((1 - c) * half + g * lanes, (1 - c) * half + (g + 1) * lanes)
                    attended[:, at] = there_ref[g]

        for n in range(0, D, 256):
            branch[:, n : n + 256] = nn(attended[...], matrix_ref[:, n : n + 256])
        bias, gain, shift = vector_ref[2:3], vector_ref[3:4], vector_ref[4:5]
        for at in row_blocks(rows):
            hidden = input_ref[at].astype(F32) + branch[at] + bias
            standardized, deviation = standardize(hidden)
            result = standardized * gain + shift
            normed[at] = result
            standard[at] = standardized
            inverse[at] = jnp.broadcast_to(deviation, (32, 128))
            low[at] = result.astype(BF)

    return block_call(
        kernel,
        "out_norm",
        [
            shaped((rows, D), F32),
            shaped((rows, D), F32),
            shaped((rows, 128), F32),
            shaped((rows, D)),
            shaped((rows, D)),
        ],
        [core],
        [here, there, inputs, vectors, matrix],
        [],
        [pltpu.VMEM((rows, D), F32)],
        2 * rows * D * D,
    )


def feed_forward(table, back_table, low_own, low_other, bias, in_parts, back_parts):
    rows = low_own.shape[0]
    units = bias.shape[1]
    chips = table.shape[0]
    tile = 256

    def kernel(table_ref, back_ref, own_ref, other_ref, bias_ref, *refs):
        n = len(in_parts)
        parts, back, refs = refs[:n], refs[n : 2 * n], refs[2 * n :]
        fed_own, fed_other, active, slope, low, in_mat, back_here, sems = refs
        first = Fetch(table_ref, parts, (0, units), in_mat, sems.at[0])
        second = Fetch(back_ref, back, (0, D), back_here, sems.at[1])
        first.start()
        second.start()
        low[:rows] = own_ref[...]
        low[rows:] = other_ref[...]
        first.wait()
        for t in range(0, units, tile):
            at = slice(t, t + tile)
            inner = nn(low[...], in_mat[:, at]) + bias_ref[:, at]
            share = 0.5 + 0.5 * lax.erf(inner * (0.5**0.5))
            active[:, at] = (inner * share).astype(BF)
            bell = jnp.exp(inner * inner * -0.5) * (1.0 / (2.0 * np.pi) ** 0.5)
            slope[:, at] = (share + inner * bell).astype(BF)
        second.wait()
        for n in range(0, D, tile):
            at = slice(n, n + tile)
            fed = nn(active[...], back_here[:, at])
            fed_own[:, at] = fed[:rows]
            fed_other[:, at] = fed[rows:].astype(BF)

    return block_call(
        kernel,
        "feed_forward",
        [
            shaped((rows, D), F32),
            shaped((rows, D)),
            shaped((2 * rows, units)),
            shaped((2 * rows, units)),
        ],
        [table, back_table],
        [low_own, low_other, bias],
        [*in_parts, *back_parts],
        [
            pltpu.VMEM((2 * rows, D), BF),
            pltpu.VMEM((D, units), BF),
            pltpu.VMEM((units, D), BF),
            pltpu.SemaphoreType.DMA((2, chips)),
        ],
        8 * rows * D * units,
    )


def last_norm(normed, fed_own, fed_there, vectors, cotangent):
    rows = normed.shape[0]

    def kernel(normed_ref, own_ref, there_ref, vector_ref, up_ref, result, grad, low, sums):
        bias, gain, shift = vector_ref[5:6], vector_ref[6:7], vector_ref[7:8]
        totals = [jnp.zeros((8, D), F32) for _ in range(3)]
        for at in row_blocks(rows):
            hidden = normed_ref[at] + own_ref[at] + there_ref[at].astype(F32) + bias
            standardized, deviation = standardize(hidden)
            result[at] = (standardized * gain + shift).astype(BF)
            up = up_ref[at].astype(F32)
            down = norm_backward(up, standardized, deviation, gain)
            grad[at] = down
            down_low = down.astype(BF)
            low[at] = down_low
            for n, term in enumerate((up * standardized, up, down_low.astype(F32))):
                totals[n] = totals[n] + fold(term, jnp.add)
        sums[...] = jnp.concatenate(
            [jnp.sum(total, 0, keepdims=True) for total in totals] + [jnp.zeros((5, D), F32)],
            axis=0,
        )

    return block_call(
        kernel,
        "last_norm",
        [shaped((rows, D)), shaped((rows, D), F32), shaped((rows, D)), shaped((8, D), F32)],
        [],
        [normed, fed_own, fed_there, vectors, cotangent],
        [],
        [],
        64 * rows * D,
    )


def place_pieces(value, first, rows, table_ref, keep, away, columns, at_row=0):
    half = keep.shape[0]
    for q in range(value.shape[0] // rows):
        place = table_ref[first + q]
        piece = value[q * rows : (q + 1) * rows].astype(BF)

        @pl.when(place < half)
        def _():
            keep[place, at_row : at_row + rows, columns] = piece

        @pl.when(place >= half)
        def _():
            away[place - half, at_row : at_row + rows, columns] = piece


def grad_back(table, active, up_own, up_other):
    rows = up_own.shape[0]
    units = active.shape[1]
    chips = table.shape[0]
    part = units // chips
    tile = 256

    def kernel(table_ref, active_ref, own_ref, other_ref, keep, away, up):
        up[:rows] = own_ref[...]
        up[rows:] = other_ref[...]
        for t in range(0, units, tile):
            value = tn(active_ref[:, t : t + tile], up[...])
            place_pieces(value, t // part, part, table_ref, keep, away, slice(0, D))

    return block_call(
        kernel,
        "grad_back",
        [shaped((chips // 2, part, D))] * 2,
        [table],
        [active, up_own, up_other],
        [],
        [pltpu.VMEM((2 * rows, D), BF)],
        4 * rows * units * D,
    )


def feed_backward(table, back_table, up_own, up_other, slope, in_parts, back_parts):
    rows = up_own.shape[0]
    units = slope.shape[1]
    chips = table.shape[0]
    tile = 256

    def kernel(table_ref, back_ref, own_ref, other_ref, slope_ref, *refs):
        n = len(in_parts)
        parts, back, refs = refs[:n], refs[n : 2 * n], refs[2 * n :]
        down_own, down_other, grad_inner, bias, up, in_mat, back_here, sems = refs
        first = Fetch(table_ref, parts, (0, units), in_mat, sems.at[0])
        second = Fetch(back_ref, back, (0, D), back_here, sems.at[1])
        second.start()
        first.start()
        up[:rows] = own_ref[...]
        up[rows:] = other_ref[...]
        second.wait()
        for t in range(0, units, tile):
            at = slice(t, t + tile)
            inner = (nt(up[...], back_here[at]) * slope_ref[:, at].astype(F32)).astype(BF)
            grad_inner[:, at] = inner
            bias[:, at] = jnp.sum(fold(inner.astype(F32), jnp.add), 0, keepdims=True)
        first.wait()
        for n in range(0, D, tile):
            at = slice(n, n + tile)
            down = nt(grad_inner[...], in_mat[at])
            down_own[:, at] = down[:rows]
            down_other[:, at] = down[rows:].astype(BF)

    return block_call(
        kernel,
        "feed_backward",
        [
            shaped((rows, D), F32),
            shaped((rows, D)),
            shaped((2 * rows, units)),
            shaped((1, units), F32),
        ],
        [table, back_table],
        [up_own, up_other, slope],
        [*in_parts, *back_parts],
        [
            pltpu.VMEM((2 * rows, D), BF),
            pltpu.VMEM((D, units), BF),
            pltpu.VMEM((units, D), BF),
            pltpu.SemaphoreType.DMA((2, chips)),
        ],
        8 * rows * D * units,
    )


def out_norm_backward(
    core, grad_two, down_own, down_there, standard, inverse, vectors, attended, matrix
):
    rows = grad_two.shape[0]
    half = D // 2
    lanes = 128 if half % 128 == 0 else half

    def kernel(
        core_ref,
        two_ref,
        own_ref,
        there_ref,
        standard_ref,
        inverse_ref,
        vector_ref,
        attended_ref,
        matrix_ref,
        grad_one,
        low,
        sums,
        grad_heads,
        grad_far,
    ):
        gain = vector_ref[3:4]
        totals = [jnp.zeros((8, D), F32) for _ in range(3)]
        for at in row_blocks(rows):
            grad = two_ref[at] + own_ref[at] + there_ref[at].astype(F32)
            standardized = standard_ref[at]
            down = norm_backward(grad, standardized, inverse_ref[at, :1], gain)
            grad_one[at] = down
            down_low = down.astype(BF)
            low[at] = down_low
            for n, term in enumerate((grad * standardized, grad, down_low.astype(F32))):
                totals[n] = totals[n] + fold(term, jnp.add)
        sums[...] = jnp.concatenate(
            [jnp.sum(total, 0, keepdims=True) for total in totals] + [jnp.zeros((5, D), F32)],
            axis=0,
        )
        for n in range(0, D, 256):
            grad_heads[:, n : n + 256] = nt(low[...], matrix_ref[n : n + 256]).astype(BF)
        yours = pl.ds(pl.multiple_of((1 - core_ref[0]) * half, half), half)
        for n in range(0, D, 256):
            grad_far[n : n + 256] = tn(attended_ref[:, n : n + 256], low[:, yours]).astype(BF)

    return block_call(
        kernel,
        "out_norm_backward",
        [
            shaped((rows, D), F32),
            shaped((rows, D)),
            shaped((8, D), F32),
            shaped((rows, D)),
            shaped((D, half)),
        ],
        [core],
        [grad_two, down_own, down_there, standard, inverse, vectors, attended, matrix],
        [],
        [],
        3 * rows * D * D,
    )


def grad_in(table, low_own, low_other, grad_inner):
    rows = low_own.shape[0]
    units = grad_inner.shape[1]
    chips = table.shape[0]
    shard = D // chips
    tile = 256

    def kernel(table_ref, own_ref, other_ref, inner_ref, keep, away, low):
        low[:rows] = own_ref[...]
        low[rows:] = other_ref[...]
        for t in range(0, D, tile):
            value = tn(low[:, t : t + tile], inner_ref[...])
            place_pieces(value, t // shard, shard, table_ref, keep, away, slice(0, units))

    return block_call(
        kernel,
        "grad_in",
        [shaped((chips // 2, shard, units))] * 2,
        [table],
        [low_own, low_other, grad_inner],
        [],
        [pltpu.VMEM((2 * rows, D), BF)],
        4 * rows * units * D,
    )


def grad_out(core, table, attended, low_grad, far):
    chips = table.shape[0]
    shard = D // chips
    half = D // 2
    tile = 256

    def kernel(core_ref, table_ref, attended_ref, grad_ref, far_ref, keep, away):
        mine = pl.ds(pl.multiple_of(core_ref[0] * half, half), half)
        for t in range(0, D, tile):
            at = slice(t, t + tile)
            value = tn(attended_ref[:, at], grad_ref[:, mine]) + far_ref[at].astype(F32)
            place_pieces(value, t // shard, shard, table_ref, keep, away, slice(0, half))

    return block_call(
        kernel,
        "grad_out",
        [shaped((chips // 2, shard, half))] * 2,
        [core, table],
        [attended, low_grad, far],
        [],
        [],
        attended.shape[0] * D * D,
    )


def grad_projections(
    numbers, table, tokens_own, tokens_other, down_own, down_other, sums_one, sums_two, in_bias, extra
):
    half, rows, width = down_own.shape
    lanes = width // 3
    chips = table.shape[0]
    shard = D // chips
    units = in_bias.shape[1]
    part = units // chips
    tile = 256

    def kernel(
        number_ref,
        table_ref,
        x_own,
        x_other,
        own_ref,
        other_ref,
        one_ref,
        two_ref,
        bias_ref,
        keep,
        away,
    ):
        own = own_ref[...].reshape(half * rows, width)
        other = other_ref[...].reshape(half * rows, width)
        for t in range(0, D, tile):
            value = jnp.zeros((tile, width), F32)
            for p in range(half):
                value = value + tn(x_own[p, :, t : t + tile], own_ref[p])
                value = value + tn(x_other[p, :, t : t + tile], other_ref[p])
            place_pieces(value, t // shard, shard, table_ref, keep, away, slice(0, width))
        totals = jnp.sum(
            fold(own.astype(F32), jnp.add) + fold(other.astype(F32), jnp.add),
            0,
            keepdims=True,
        )
        pair = jnp.concatenate([totals[:, :lanes], totals[:, 2 * lanes :]], axis=0)
        pair = jnp.concatenate(
            [jnp.where(number_ref[1] == a, pair, 0.0) for a in range(D // lanes)], axis=1
        )
        one, two = one_ref[...], two_ref[...]
        stacked = jnp.concatenate(
            [pair, one[2:3], one[0:1], one[1:2], two[2:3], two[0:1], two[1:2]], axis=0
        )
        blank = jnp.zeros((1, part), F32)
        for i in range(chips):
            bias = bias_ref[:, i * part : (i + 1) * part]
            bias = jnp.where(
                number_ref[0] == 0,
                jnp.concatenate([bias, blank], axis=1),
                jnp.concatenate([blank, bias], axis=1),
            )
            top = stacked[:, i * shard : (i + 1) * shard]
            rest = extra - 9
            block = jnp.concatenate(
                [
                    jnp.concatenate([top, jnp.zeros((8, width - shard), F32)], axis=1),
                    jnp.concatenate([bias, jnp.zeros((1, width - 2 * part), F32)], axis=1),
                    jnp.zeros((rest, width), F32),
                ],
                axis=0,
            )
            place_pieces(block, i, extra, table_ref, keep, away, slice(0, width), shard)

    return block_call(
        kernel,
        "grad_projections",
        [shaped((chips // 2, shard + extra, width))] * 2,
        [numbers, table],
        [
            tokens_own,
            tokens_other,
            down_own,
            down_other,
            sums_one,
            sums_two,
            in_bias,
        ],
        [],
        [],
        4 * half * rows * D * width,
    )


def pack(numbers, weights, vectors, bias, marks, groups, extra):
    shard = weights[0].shape[0]
    half = D // 2
    lanes = half // groups
    width = 3 * lanes

    def kernel(number_ref, *refs):
        *weight_refs, vector_ref, bias_ref, mark_ref, out = refs

        def lines(row):
            count = -(-row.shape[1] // width)
            padded = jnp.concatenate(
                [row, jnp.zeros((1, count * width - row.shape[1]), F32)], axis=1
            )
            return [padded[:, n * width : (n + 1) * width] for n in range(count)]

        small = vector_ref[...].astype(F32)
        block = [jnp.concatenate([small, jnp.zeros((8, width - small.shape[1]), F32)], axis=1)]
        block += lines(bias_ref[...].astype(F32)) + lines(mark_ref[...].astype(F32))
        filled = 8 + len(block) - 1
        block = jnp.concatenate(block + [jnp.zeros((extra - filled, width), F32)], axis=0)
        block = block.astype(BF)
        for d in range(groups):
            out[d, shard:] = block
        for c in range(2):

            @pl.when(number_ref[0] == c)
            def _():
                for a in range(groups):
                    place = number_ref[2 + a]
                    for n, weight in enumerate(weight_refs):
                        start = c * half + a * lanes
                        out[place, :shard, n * lanes : (n + 1) * lanes] = weight[
                            :, start : start + lanes
                        ]

    return block_call(
        kernel,
        "pack",
        [shaped((groups, shard + extra, width))],
        [numbers],
        [*weights, vectors, bias, marks],
        [],
        [],
        0,
    )[0]


def send(value, perm):
    return lax.ppermute(value, AXES, perm)


def gather_stages(block, perms):
    for perm in perms[:-1]:
        block = jnp.concatenate([block, send(block, perm)], axis=0)
    return [block, send(block, perms[-1])]


def hold(value, *earlier):
    return lax.optimization_barrier((value, *earlier))[0]


class Gather:
    def __init__(self, block, perms):
        self.parts, self.perms = [block], perms

    def block(self, *earlier):
        parts = lax.optimization_barrier((*self.parts, *earlier))[: len(self.parts)]
        return jnp.concatenate(parts, axis=0) if len(parts) > 1 else parts[0]

    def stage(self, *earlier):
        block = self.block(*earlier)
        self.parts = [block, send(block, self.perms[0])]
        self.perms = self.perms[1:]
        return self.parts[1]


class Scatter:
    def __init__(self, keep, away, perms):
        self.keep, self.away, self.perms = keep, away, perms[::-1]

    def stage(self, *earlier):
        arrived = send(self.away, self.perms[0])
        arrived = hold(arrived, *earlier) if earlier else arrived
        self.perms = self.perms[1:]
        if self.perms:
            half = self.keep.shape[0] // 2
            self.away = self.keep[half:] + arrived[half:]
            self.keep = self.keep[:half] + arrived[:half]
        else:
            self.keep = self.keep.astype(F32) + arrived.astype(F32)
        return arrived

    def finish(self):
        while self.perms:
            self.stage()
        return self.keep


def pieces(count, rows, columns):
    return jax.ShapeDtypeStruct((count, rows, columns), BF)


def body(
    plan,
    tokens,
    segment_ids,
    w_query,
    b_query,
    w_key,
    w_value,
    b_value,
    w_out,
    b_out,
    g_attn,
    n_attn,
    w_in,
    b_in,
    w_back,
    b_back,
    g_ffn,
    n_ffn,
    cotangent,
):
    chips, groups, heads, ctx = plan.chips, plan.groups, plan.heads, plan.ctx
    core = lax.axis_index("dp")
    place = lax.axis_index("ctx")
    device = (core * ctx + place) * plan.fsdp + lax.axis_index("fsdp")
    side, group = place // groups, place % groups
    rows = tokens.shape[1]
    shard = w_query.shape[0]
    hidden = w_back.shape[0]
    part = hidden // 2
    units = FF // 2
    lanes = heads * HD
    half_d = D // 2
    width = 3 * lanes
    bias_rows, mark_rows = -(-hidden // width), -(-rows // width)
    extra = 16 * (-(-(8 + bias_rows + mark_rows) // 16))
    swap = plan.core_swap()
    in_perms = plan.chip_perms(plan.in_orders)
    back_perms = plan.chip_perms(plan.back_orders)

    side_table = plan.side_pieces()
    tables = dict(
        w_in=plan.chip_gather(plan.in_orders),
        w_back=plan.chip_gather(plan.back_orders),
        pieces=invert(side_table),
        chunks=plan.table(lambda c, j, f: [plan.chunk_of(c, j, p) for p in range(ctx)]),
        numbers=plan.table(
            lambda c, j, f: [c, c * groups + j % groups]
            + [a ^ (j % groups) for a in range(groups)]
        ),
    )
    table_row = lax.dynamic_index_in_dim(
        jnp.asarray(np.concatenate(list(tables.values()), axis=1)), device, 0, False
    )
    starts = np.cumsum([0] + [t.shape[1] for t in tables.values()])
    look = {
        name: table_row[starts[n] : starts[n + 1]] for n, name in enumerate(tables)
    }

    def mine(columns, size, axis=1):
        return lax.dynamic_slice_in_dim(columns, core * size, size, axis)

    w_in_mine = lax.dynamic_index_in_dim(
        w_in.reshape(shard, chips, 2, part), core, 2, False
    ).reshape(1, shard, units)
    w_back_mine = mine(w_back, part, 0)[None]
    in_gather = Gather(w_in_mine, in_perms)
    back_gather = Gather(w_back_mine, back_perms)
    out_gather = Gather(mine(w_out, half_d)[None], in_perms)

    inputs = tokens[0]
    turned = send(inputs, plan.turn())
    block = turned[None]
    reached = [turned]
    for perm in plan.group_perms():
        reached.append(send(block, perm))
        block = jnp.concatenate([block, reached[-1]], axis=0)
    tokens_own = block
    tokens_other = send(tokens_own, swap)
    in_gather.stage(turned)
    in_gather.stage(reached[1])
    back_gather.stage(reached[1])
    out_gather.stage(reached[1])
    in_gather.stage(reached[2])
    back_gather.stage(reached[2])
    out_gather.stage(reached[2])

    vectors = jnp.stack([b_query, b_value, b_out, g_attn, n_attn, b_back, g_ffn, n_ffn])
    messages = pack(
        look["numbers"],
        [w_query, w_key, w_value],
        vectors,
        b_in[None],
        segment_ids,
        groups,
        extra,
    )
    arrived = [messages[0]] + [
        send(messages[d], plan.group_direct(d)) for d in range(1, groups)
    ]
    gathered = gather_stages(hold(jnp.stack(arrived), turned), plan.side_perms())
    heads_mat, extras = route(
        gathered,
        look["pieces"],
        [pieces(chips, shard, width), pieces(chips, extra, width)],
        [((0, 1), i, 0, shard, 0, i, 0) for i in range(chips)]
        + [((0, 1), i, shard, extra, 1, i, 0) for i in range(chips)],
    )
    heads_mat = heads_mat.reshape(D, width)
    vectors = extras[:, :8, :shard].transpose(1, 0, 2).reshape(8, D).astype(F32)
    in_bias = extras[:, 8 : 8 + bias_rows].reshape(chips, -1)[:, :hidden]
    in_bias = (
        lax.dynamic_slice_in_dim(in_bias, core * part, part, 1).reshape(1, units).astype(F32)
    )
    at = 8 + bias_rows
    ids_here = extras[:, at : at + mark_rows].reshape(chips, -1)[:, :rows]
    ids_here = lax.dynamic_index_in_dim(
        ids_here.reshape(ctx, plan.fsdp, rows), lax.axis_index("fsdp"), 1, False
    )
    ids_there = send(ids_here, swap)
    ids_all = jnp.where(core == side, ids_here, ids_there).astype(F32)
    chosen = look["chunks"][:, None] == jnp.arange(ctx)[None]
    ids = jnp.sum(jnp.where(chosen[:, :, None], ids_all[None], 0.0), axis=1)
    first, last = ids[:, 0], ids[:, -1]
    overlap = ((first[:, None] <= last[None]) & (first[None] <= last[:, None])).astype(jnp.int32)
    ids = ids[:, None, :]
    meets = listing(overlap)

    start = core * half_d + group * lanes
    heads_bias = jnp.concatenate(
        [
            lax.dynamic_slice(vectors, (0, start), (1, lanes)),
            jnp.zeros((1, lanes), F32),
            lax.dynamic_slice(vectors, (1, start), (1, lanes)),
        ],
        axis=1,
    )

    def project(block):
        return (
            jnp.einsum("ptd,dw->ptw", block, heads_mat, preferred_element_type=F32) + heads_bias
        ).astype(BF)

    qkv_own, qkv_other = project(tokens_own), project(tokens_other)
    in_gather.stage(qkv_own)
    in_parts = in_gather.parts
    back_gather.stage(qkv_own)
    out_gather.stage(qkv_own)
    qkv_other = hold(qkv_other, in_parts[0], back_gather.parts[0])
    sent, flat, totals = attend_forward(
        look["chunks"], qkv_own, qkv_other, ids, meets, heads
    )
    met = lax.all_to_all(sent, "ctx", 0, 0, tiled=True).reshape(2, groups, rows, lanes)
    back_gather.stage(sent, in_parts[1])
    back_parts = back_gather.parts
    out_gather.stage(sent)
    out_parts = out_gather.parts
    (out_mine,) = route(
        out_parts,
        look["w_in"],
        [pieces(chips, shard, half_d)],
        [((0, 1), i, 0, shard, 0, i, 0) for i in range(chips)],
    )
    out_mine = out_mine.reshape(D, half_d)
    out_there = send(out_mine, swap)
    out_mat = jnp.where(
        core == 0,
        jnp.concatenate([out_mine, out_there], axis=1),
        jnp.concatenate([out_there, out_mine], axis=1),
    )
    here = lax.dynamic_index_in_dim(met, core, 0, False)
    there = send(lax.dynamic_index_in_dim(met, 1 - core, 0, False), swap)

    core_number = look["numbers"][:1]
    normed, standard, inverse, low_own, attended = out_norm(
        core_number, here, there, inputs, vectors, out_mat
    )
    low_other = send(low_own, swap)
    fed_own, fed_other, active, slope = feed_forward(
        look["w_in"], look["w_back"], low_own, low_other, in_bias, in_parts, back_parts
    )
    result, grad_two, up_own, sums_two = last_norm(
        normed, fed_own, send(fed_other, swap), vectors, cotangent[0]
    )
    up_other = send(up_own, swap)
    back_scatter = Scatter(*grad_back(look["w_back"], active, up_own, up_other), back_perms)
    down_own, down_other, grad_inner, grad_in_bias = feed_backward(
        look["w_in"],
        look["w_back"],
        hold(up_own, back_scatter.away),
        up_other,
        slope,
        in_parts,
        back_parts,
    )
    in_scatter = Scatter(*grad_in(look["w_in"], low_own, low_other, grad_inner), in_perms)
    grad_one, low_grad, sums_one, grad_heads, grad_far = out_norm_backward(
        core_number,
        hold(grad_two, in_scatter.away),
        down_own,
        send(down_other, swap),
        standard,
        inverse,
        vectors,
        attended,
        out_mat,
    )
    grad_heads = grad_heads.reshape(rows, 2, groups, lanes).transpose(1, 2, 0, 3)
    kept = lax.dynamic_index_in_dim(grad_heads, core, 0, False)
    towards = send(lax.dynamic_index_in_dim(grad_heads, 1 - core, 0, False), swap)
    grad_heads = jnp.where(
        core == 0, jnp.stack([kept, towards]), jnp.stack([towards, kept])
    ).reshape(ctx, rows, lanes)
    grads = lax.all_to_all(grad_heads, "ctx", 0, 0, tiled=True)
    out_scatter = Scatter(
        *grad_out(
            core_number,
            look["w_in"],
            hold(attended, grad_heads),
            low_grad,
            send(grad_far, swap),
        ),
        in_perms,
    )

    back_scatter.stage(grad_heads)
    in_scatter.stage(back_scatter.away)
    grads = hold(grads, back_scatter.away, in_scatter.away, out_scatter.away)
    back_second = back_scatter.stage()
    in_second = in_scatter.stage()
    qkv_grads = attend_backward(
        look["chunks"], qkv_own, qkv_other, ids, meets, grads, flat, totals, heads
    )
    qkv_grads = lax.optimization_barrier((*qkv_grads, back_second, in_second))[:2]
    down_own, down_other = qkv_grads

    def back_project(down):
        return jnp.einsum("ptw,dw->ptd", down, heads_mat, preferred_element_type=F32)

    towards = send(back_project(down_other).astype(BF), swap)
    block = (back_project(down_own) + towards.astype(F32)).astype(BF)
    down_own, down_other, _ = lax.optimization_barrier((down_own, down_other, block))
    side_scatter = Scatter(
        *grad_projections(
            look["numbers"],
            look["pieces"],
            tokens_own,
            tokens_other,
            down_own,
            down_other,
            sums_one,
            sums_two,
            grad_in_bias,
            extra,
        ),
        plan.side_perms(),
    )
    reached = []
    for perm in plan.group_perms()[::-1]:
        half = block.shape[0] // 2
        reached.append(send(block[half:], perm))
        block = block[:half] + reached[-1]
    in_scatter.stage(reached[0])
    back_scatter.stage(reached[0])
    out_scatter.stage(reached[0])
    side_scatter.stage(reached[-1])
    ended = send(block[0], plan.turn())
    side_last = send(side_scatter.away, side_scatter.perms[0])
    low_by_group = (side_scatter.keep + side_last)
    out_scatter.stage(reached[-1])
    back_last = back_scatter.finish()
    grad_back_mat = hold(back_last[0], reached[-1])
    grad_inputs = grad_one + ended.astype(F32)
    in_last = in_scatter.finish()
    in_scatter.keep = hold(in_last, reached[-1])
    by_group = [low_by_group[0]] + [
        send(low_by_group[d], plan.group_direct(d)) for d in range(1, groups)
    ]
    by_group = jnp.stack(by_group).astype(F32)
    grad_extras = jnp.sum(by_group[:, shard:], 0)
    grad_columns = jnp.stack(
        [lax.dynamic_index_in_dim(by_group, group ^ d, 0, False)[:shard] for d in range(groups)]
    )
    grad_columns = grad_columns.reshape(groups, shard, 3, lanes).transpose(2, 1, 0, 3)
    grad_columns = grad_columns.reshape(3, shard, half_d)
    grad_in_mat = in_scatter.finish()[0]
    grad_out_mat = out_scatter.finish()[0]

    def both(half, axis):
        there = send(half, swap)
        return jnp.where(
            core == 0, jnp.stack([half, there], axis=axis), jnp.stack([there, half], axis=axis)
        )

    grad_columns = both(grad_columns, 2).reshape(3, shard, D)
    grad_out_mat = both(grad_out_mat, 1).reshape(shard, D)
    grad_in_mat = both(grad_in_mat.reshape(shard, chips, part), 2).reshape(
        shard, FF
    )
    grad_back_mat = both(grad_back_mat, 0).reshape(hidden, D)
    sums = grad_extras + send(grad_extras, swap)
    small = [sums[which, :shard] for which in range(8)]
    return (
        result[None],
        grad_inputs[None],
        grad_columns[0],
        small[0],
        grad_columns[1],
        grad_columns[2],
        small[1],
        grad_out_mat,
        small[2],
        small[3],
        small[4],
        grad_in_mat,
        sums[8:].reshape(-1)[:hidden],
        grad_back_mat,
        small[5],
        small[6],
        small[7],
    )


def solution(mesh):
    owned = ("ctx", "fsdp")
    matrix, vector = P(owned, None), P(owned)
    sequence = P(("dp", "fsdp"), "ctx", None)
    return jax.shard_map(
        partial(body, Plan(mesh)),
        mesh=mesh,
        in_specs=(
            sequence,
            P(("dp", "fsdp"), "ctx"),
            matrix,
            vector,
            matrix,
            matrix,
            vector,
            matrix,
            vector,
            vector,
            vector,
            matrix,
            vector,
            matrix,
            vector,
            vector,
            vector,
            sequence,
        ),
        out_specs=(
            sequence,
            sequence,
            matrix,
            vector,
            matrix,
            matrix,
            vector,
            matrix,
            vector,
            vector,
            vector,
            matrix,
            vector,
            matrix,
            vector,
            vector,
            vector,
        ),
        check_vma=False,
    )
```

```python
from functools import partial

import jax
import jax.numpy as jnp
import numpy as np
from jax import lax
from jax.experimental import pallas as pl
from jax.experimental.pallas import tpu as pltpu
from jax.sharding import PartitionSpec as P

D = 1024
H = 16
HD = 64
FF = 4096
NORM_EPS = 1e-05
NEG_FILL = -1e30
AXES = ("dp", "ctx", "fsdp")
BF = jnp.bfloat16
F32 = jnp.float32
VMEM_LIMIT = 48 * 1024 * 1024


def subset_masks(order):
    table = [0]
    for mask in order:
        table = table + [mask ^ entry for entry in table]
    return table


def bits_of(count):
    return [1 << t for t in range(count.bit_length() - 1)]


class Plan:
    def __init__(self, mesh):
        self.ctx = mesh.shape["ctx"]
        self.fsdp = mesh.shape["fsdp"]
        self.chips = self.ctx * self.fsdp
        self.groups = self.ctx // 2
        self.heads = H // self.ctx
        self.devices = [
            (c, j, f) for c in range(2) for j in range(self.ctx) for f in range(self.fsdp)
        ]
        bits = bits_of(self.chips)
        self.in_orders = [bits[:1:-1] + [1, 2], bits[:1:-1] + [2, 1]]
        self.back_orders = self.in_orders
        group_bits = bits_of(self.groups)
        self.group_orders = [group_bits[::-1], group_bits]
        self.group_masks = [subset_masks(order) for order in self.group_orders]
        top = self.groups * self.fsdp
        self.side_orders = [[top] + bits_of(self.fsdp)] * 2
        self.side_masks = [subset_masks(order) for order in self.side_orders]

    def flat(self, c, j, f):
        return (c * self.ctx + j) * self.fsdp + f

    def perm(self, move):
        return [(self.flat(*dev), self.flat(*move(*dev))) for dev in self.devices]

    def chip_xor(self, masks):
        def move(c, j, f):
            i = (j * self.fsdp + f) ^ masks[c]
            return (c, i // self.fsdp, i % self.fsdp)

        return self.perm(move)

    def chip_perms(self, orders):
        return [self.chip_xor(pair) for pair in zip(*orders)]

    def side_perms(self):
        return [self.chip_xor(pair) for pair in zip(*self.side_orders)]

    def group_perms(self):
        return [
            self.perm(lambda c, j, f, pair=pair: (c, j ^ pair[c], f))
            for pair in zip(*self.group_orders)
        ]

    def group_direct(self, d):
        return self.perm(lambda c, j, f: (c, j ^ d, f))

    def core_swap(self):
        return self.perm(lambda c, j, f: (1 - c, j, f))

    def turn(self):
        def move(c, j, f):
            return (j // self.groups, c * self.groups + j % self.groups, f)

        return self.perm(move)

    def chunk_of(self, c, j, p):
        e, k = divmod(p, self.groups)
        return (c ^ e) * self.groups + ((j % self.groups) ^ self.group_masks[c ^ e][k])

    def table(self, entries):
        return np.array([entries(*dev) for dev in self.devices], np.int32)

    def chip_gather(self, orders):
        def entries(c, j, f):
            inverse = np.argsort(subset_masks(orders[c]))
            return [inverse[(j * self.fsdp + f) ^ i] for i in range(self.chips)]

        return self.table(entries)

    def other_core(self, table):
        return table.reshape(2, -1, table.shape[1])[::-1].reshape(table.shape)

    def side_pieces(self):
        def entries(c, j, f):
            return [
                (j * self.fsdp + f) ^ mask ^ (d * self.fsdp)
                for mask in self.side_masks[c]
                for d in range(self.groups)
            ]

        return self.table(entries)


def invert(table):
    return np.argsort(table, axis=1).astype(np.int32)


def route(sources, table, outs, moves):
    def kernel(table_ref, *refs):
        ins, results, sems = refs[: len(sources)], refs[len(sources) : -1], refs[-1]

        def copy(m, source, piece):
            _, _, row, rows, out, out_piece, out_row = moves[m]
            return pltpu.make_async_copy(
                source.at[piece, pl.ds(row, rows)],
                results[out].at[out_piece, pl.ds(out_row, rows)],
                sems.at[m],
            )

        for m, (group, slot, *_) in enumerate(moves):
            index = table_ref[slot]
            start = 0
            for which in group:
                count = sources[which].shape[0]

                @pl.when((index >= start) & (index < start + count))
                def _():
                    copy(m, ins[which], index - start).start()

                start += count
        for m, (group, *_) in enumerate(moves):
            copy(m, ins[group[0]], 0).wait()

    total = sum(
        moves[m][3] * outs[moves[m][4]].shape[2] * outs[moves[m][4]].dtype.itemsize
        for m in range(len(moves))
    )
    return pl.pallas_call(
        kernel,
        out_shape=outs,
        in_specs=[pl.BlockSpec(memory_space=pltpu.SMEM)]
        + [pl.BlockSpec(memory_space=pl.ANY)] * len(sources),
        out_specs=[pl.BlockSpec(memory_space=pltpu.VMEM)] * len(outs),
        scratch_shapes=[pltpu.SemaphoreType.DMA((len(moves),))],
        compiler_params=pltpu.CompilerParams(vmem_limit_bytes=VMEM_LIMIT),
        cost_estimate=pl.CostEstimate(flops=0, bytes_accessed=0, transcendentals=0),
    )(table, *sources)


def nt(left, right):
    return lax.dot_general(left, right, (((1,), (1,)), ((), ())), preferred_element_type=F32)


def nn(left, right):
    return lax.dot_general(left, right, (((1,), (0,)), ((), ())), preferred_element_type=F32)


def tn(left, right):
    return lax.dot_general(left, right, (((0,), (0,)), ((), ())), preferred_element_type=F32)


def column_ids(row):
    return jnp.transpose(jnp.broadcast_to(row, (128, row.shape[1])))


def listing(overlap):
    count = overlap.shape[0]
    before = jnp.arange(count)[None, :] < jnp.arange(count)[:, None]
    rank = jnp.sum(jnp.where(before[None], overlap[:, None, :], 0), 2)
    slot = jnp.where(overlap > 0, rank, count)
    here = slot[:, None, :] == jnp.arange(count)[None, :, None]
    order = jnp.sum(jnp.where(here, jnp.arange(count)[None, None, :], 0), 2)
    return jnp.concatenate([order, jnp.sum(overlap, 1, keepdims=True)], 1).astype(jnp.int32)


def fold(values, combine):
    rows = values.shape[0]
    while rows > 8:
        rows //= 2
        values = combine(values[:rows], values[rows:])
    return values


def looped(count, step, carry):
    pairs = count // 2
    carry = lax.fori_loop(0, pairs, lambda t, c: step(2 * t + 1, step(2 * t, c)), carry)
    return lax.fori_loop(2 * pairs, count, step, carry)


def same_document(columns, row):
    repeats = -(-columns.shape[0] // 128)
    return jnp.concatenate([columns] * repeats, axis=1)[:, : row.shape[1]] == row


def one_head(flat, h, heads):
    zero = jnp.zeros((HD, flat.shape[1]), flat.dtype)
    return jnp.concatenate(
        [flat[g * HD : (g + 1) * HD] if g == h else zero for g in range(heads)], axis=0
    )


def attend_forward(places, qkv_own, qkv_other, ids, meets, heads):
    half, rows, width = qkv_own.shape
    chunks = 2 * half
    lanes = heads * HD

    def kernel(list_ref, place_ref, own_ref, other_ref, ids_ref, *refs):
        out_ref, flat_ref, total_ref, keys, values, queries, cols, logits_ref = refs
        step = pl.program_id(0)

        @pl.when(step == 0)
        def _():
            for p in range(chunks):
                block = (own_ref if p < half else other_ref)[p % half]
                query = jnp.transpose(block[:, :lanes] * BF(HD**-0.5))
                for h in range(heads):
                    queries[p, h] = one_head(query, h, heads)
                keys[p] = block[:, lanes : 2 * lanes]
                values[p] = jnp.transpose(block[:, 2 * lanes :])
                cols[p] = column_ids(ids_ref[p])

        row_ids = ids_ref[step]
        count = list_ref[step, chunks]
        query = [queries[step, h] for h in range(heads)]

        def scores(t, highs):
            p = list_ref[step, t]
            same = same_document(cols[p], row_ids)
            key = keys[p]
            new = []
            for h in range(heads):
                logits = jnp.where(same, nn(key, query[h]), NEG_FILL)
                logits_ref[h, t] = logits
                new.append(jnp.maximum(highs[h], fold(logits, jnp.maximum)))
            return tuple(new)

        highs = looped(
            count, scores, tuple(jnp.full((8, rows), NEG_FILL, F32) for _ in range(heads))
        )
        highs = [jnp.max(high, 0, keepdims=True) for high in highs]

        def attend(t, sums):
            p = list_ref[step, t]
            new = []
            for h in range(heads):
                low, acc = sums[h]
                weights = jnp.exp(logits_ref[h, t] - highs[h])
                new.append(
                    (
                        low + fold(weights, jnp.add),
                        acc + nn(values[p, h * HD : (h + 1) * HD], weights.astype(BF)),
                    )
                )
            return tuple(new)

        sums = looped(
            count,
            attend,
            tuple(
                (jnp.zeros((8, rows), F32), jnp.zeros((HD, rows), F32)) for _ in range(heads)
            ),
        )
        lows = [jnp.sum(low, 0, keepdims=True) for low, _ in sums]
        flat = jnp.concatenate([acc / low for (_, acc), low in zip(sums, lows)], axis=0)
        flat_ref[0] = flat
        total_ref[0] = jnp.concatenate(
            [high + jnp.log(low) for high, low in zip(highs, lows)]
            + [jnp.zeros((8 - heads, rows), F32)],
            axis=0,
        )
        out_ref[0] = jnp.transpose(flat).astype(BF)

    whole = lambda *shape: pl.BlockSpec(shape, lambda i, o, q: (0,) * len(shape))
    pairs = chunks * chunks * heads
    return pl.pallas_call(
        kernel,
        name="attend_forward",
        out_shape=[
            jax.ShapeDtypeStruct((chunks, rows, lanes), BF),
            jax.ShapeDtypeStruct((chunks, lanes, rows), F32),
            jax.ShapeDtypeStruct((chunks, 8, rows), F32),
        ],
        grid_spec=pltpu.PrefetchScalarGridSpec(
            num_scalar_prefetch=2,
            grid=(chunks,),
            in_specs=[
                whole(half, rows, width),
                whole(half, rows, width),
                whole(chunks, 1, rows),
            ],
            out_specs=[
                pl.BlockSpec((1, rows, lanes), lambda i, o, q: (q[i], 0, 0)),
                pl.BlockSpec((1, lanes, rows), lambda i, o, q: (i, 0, 0)),
                pl.BlockSpec((1, 8, rows), lambda i, o, q: (i, 0, 0)),
            ],
            scratch_shapes=[
                pltpu.VMEM((chunks, rows, lanes), BF),
                pltpu.VMEM((chunks, lanes, rows), BF),
                pltpu.VMEM((chunks, heads, lanes, rows), BF),
                pltpu.VMEM((chunks, rows, 128), F32),
                pltpu.VMEM((heads, chunks, rows, rows), F32),
            ],
        ),
        compiler_params=pltpu.CompilerParams(vmem_limit_bytes=VMEM_LIMIT),
        cost_estimate=pl.CostEstimate(
            flops=pairs * rows * rows * 24000,
            bytes_accessed=chunks * rows * width * 4,
            transcendentals=pairs * rows * rows,
        ),
    )(meets, places, qkv_own, qkv_other, ids)


def attend_backward(places, qkv_own, qkv_other, ids, meets, grads, flat, totals, heads):
    half, rows, width = qkv_own.shape
    chunks = 2 * half
    lanes = heads * HD

    def kernel(
        list_ref, place_ref, own_ref, other_ref, ids_ref, flat_ref, total_ref, up_ref, *refs
    ):
        down_own, down_other = refs[:2]
        keys, turned, values, queries, cols, grad_key, grad_value = refs[2:]
        step = pl.program_id(0)

        @pl.when(step == 0)
        def _():
            for p in range(chunks):
                block = (own_ref if p < half else other_ref)[p % half]
                queries[p] = block[:, :lanes] * BF(HD**-0.5)
                keys[p] = block[:, lanes : 2 * lanes]
                turned[p] = jnp.transpose(block[:, lanes : 2 * lanes])
                values[p] = block[:, 2 * lanes :]
                cols[p] = column_ids(ids_ref[p])
            grad_key[...] = jnp.zeros_like(grad_key)
            grad_value[...] = jnp.zeros_like(grad_value)

        query = queries[step]
        up = up_ref[0]
        row_ids = ids_ref[step]
        count = list_ref[step, chunks]
        query_turned, up_turned = jnp.transpose(query), jnp.transpose(up)
        product = up_turned.astype(F32) * flat_ref[0]
        deltas = [
            jnp.sum(product[h * HD : (h + 1) * HD], 0, keepdims=True) for h in range(heads)
        ]
        total = total_ref[0]
        lane_head = lax.broadcasted_iota(jnp.int32, (rows, lanes), 1) // HD
        queries_turned = [one_head(query_turned, h, heads) for h in range(heads)]
        ups_turned = [one_head(up_turned, h, heads) for h in range(heads)]
        queries_wide = [jnp.where(lane_head == h, query, BF(0)) for h in range(heads)]
        ups_wide = [jnp.where(lane_head == h, up, BF(0)) for h in range(heads)]

        def one(t, carry):
            p = list_ref[step, t]
            same = same_document(cols[p], row_ids)
            key, value = keys[p], values[p]
            sum_key, sum_value = grad_key[p], grad_value[p]
            new = []
            for h in range(heads):
                logits = jnp.where(same, nn(key, queries_turned[h]), NEG_FILL)
                weights = jnp.exp(logits - total[h : h + 1])
                grad_prob = nn(value, ups_turned[h])
                grad_score = (weights * (grad_prob - deltas[h])).astype(BF)
                sum_value = sum_value + nn(weights.astype(BF), ups_wide[h])
                sum_key = sum_key + nn(grad_score, queries_wide[h])
                new.append(carry[h] + nn(turned[p, h * HD : (h + 1) * HD], grad_score))
            grad_value[p] = sum_value
            grad_key[p] = sum_key
            return tuple(new)

        acc = looped(count, one, tuple(jnp.zeros((HD, rows), F32) for _ in range(heads)))
        grad_query = (jnp.transpose(jnp.concatenate(acc, 0)) * HD**-0.5).astype(BF)
        for p in range(chunks):
            out = down_own if p < half else down_other

            @pl.when(step == p)
            def _():
                out[p % half, :, :lanes] = grad_query

            @pl.when(step == chunks - 1)
            def _():
                out[p % half, :, lanes : 2 * lanes] = grad_key[p].astype(BF)
                out[p % half, :, 2 * lanes :] = grad_value[p].astype(BF)

    whole = lambda *shape: pl.BlockSpec(shape, lambda i, o, q: (0,) * len(shape))
    pairs = chunks * chunks * heads
    return pl.pallas_call(
        kernel,
        name="attend_backward",
        out_shape=[jax.ShapeDtypeStruct((half, rows, width), BF)] * 2,
        grid_spec=pltpu.PrefetchScalarGridSpec(
            num_scalar_prefetch=2,
            grid=(chunks,),
            in_specs=[
                whole(half, rows, width),
                whole(half, rows, width),
                whole(chunks, 1, rows),
                pl.BlockSpec((1, lanes, rows), lambda i, o, q: (i, 0, 0)),
                pl.BlockSpec((1, 8, rows), lambda i, o, q: (i, 0, 0)),
                pl.BlockSpec((1, rows, lanes), lambda i, o, q: (q[i], 0, 0)),
            ],
            out_specs=[whole(half, rows, width)] * 2,
            scratch_shapes=[
                pltpu.VMEM((chunks, rows, lanes), BF),
                pltpu.VMEM((chunks, lanes, rows), BF),
                pltpu.VMEM((chunks, rows, lanes), BF),
                pltpu.VMEM((chunks, rows, lanes), BF),
                pltpu.VMEM((chunks, rows, 128), F32),
                pltpu.VMEM((chunks, rows, lanes), F32),
                pltpu.VMEM((chunks, rows, lanes), F32),
            ],
        ),
        compiler_params=pltpu.CompilerParams(vmem_limit_bytes=VMEM_LIMIT),
        cost_estimate=pl.CostEstimate(
            flops=pairs * rows * rows * 24000,
            bytes_accessed=chunks * rows * width * 8,
            transcendentals=pairs * rows * rows,
        ),
    )(meets, places, qkv_own, qkv_other, ids, flat, totals, grads)


def block_call(kernel, name, outs, tables, blocks, hbm, scratch, flops, space=pltpu.VMEM):
    moved = sum(x.size * x.dtype.itemsize for x in (*blocks, *hbm, *outs))
    return pl.pallas_call(
        kernel,
        name=name,
        out_shape=list(outs),
        in_specs=[pl.BlockSpec(memory_space=pltpu.SMEM)] * len(tables)
        + [pl.BlockSpec(memory_space=pltpu.VMEM)] * len(blocks)
        + [pl.BlockSpec(memory_space=pl.ANY)] * len(hbm),
        out_specs=[pl.BlockSpec(memory_space=space)] * len(outs),
        scratch_shapes=list(scratch),
        compiler_params=pltpu.CompilerParams(vmem_limit_bytes=VMEM_LIMIT),
        cost_estimate=pl.CostEstimate(flops=0, bytes_accessed=0, transcendentals=0),
    )(*tables, *blocks, *hbm)


def shaped(shape, dtype=BF):
    return jax.ShapeDtypeStruct(shape, dtype)


class Fetch:
    def __init__(self, table_ref, parts, columns, target, sems, at=0):
        self.table, self.parts, self.sems = table_ref, parts, sems
        self.source = pl.ds(*columns)
        self.target, self.place = target, pl.ds(at, columns[1])
        self.rows = parts[0].shape[1]
        self.count = target.shape[0] // self.rows

    def copy(self, part, piece, i):
        rows = pl.ds(pl.multiple_of(i * self.rows, self.rows), self.rows)
        return pltpu.make_async_copy(
            part.at[piece, :, self.source], self.target.at[rows, self.place], self.sems.at[i]
        )

    def start(self):
        def one(i, carry):
            index = self.table[i]
            first = 0
            for part in self.parts:
                count = part.shape[0]

                @pl.when((index >= first) & (index < first + count))
                def _():
                    self.copy(part, index - first, i).start()

                first += count
            return carry

        lax.fori_loop(0, self.count, one, 0)

    def wait(self):
        def one(i, carry):
            self.copy(self.parts[0], 0, i).wait()
            return carry

        lax.fori_loop(0, self.count, one, 0)


def row_blocks(rows, size=32):
    return [slice(r, r + size) for r in range(0, rows, size)]


def standardize(hidden):
    centered_input = hidden - jnp.mean(hidden, -1, keepdims=True)
    inverse_deviation = lax.rsqrt(
        jnp.mean(centered_input * centered_input, -1, keepdims=True) + NORM_EPS
    )
    return centered_input * inverse_deviation, inverse_deviation


def norm_backward(upstream_gradient, standardized_input, inverse_deviation, norm_gain):
    scaled_rows = upstream_gradient * norm_gain
    return inverse_deviation * (
        scaled_rows
        - jnp.mean(scaled_rows, -1, keepdims=True)
        - standardized_input * jnp.mean(scaled_rows * standardized_input, -1, keepdims=True)
    )


def out_norm(core, near_table, far_table, here, there, inputs, vectors, near_parts, far_part, first):
    groups, rows, lanes = here.shape
    half = D // 2
    chips = near_table.shape[0]

    def kernel(
        core_ref, near_ref, far_ref, here_ref, there_ref, input_ref, vector_ref, *refs
    ):
        parts, far_part_ref = refs[: len(near_parts)], refs[len(near_parts)]
        normed, standard, inverse, low, attended, matrix, branch, sems = refs[
            len(near_parts) + 1 :
        ]
        mine = pl.multiple_of(core_ref[0] * half, half)
        yours = pl.multiple_of((1 - core_ref[0]) * half, half)
        near = Fetch(near_ref, parts, (first, half), matrix, sems.at[0], mine)
        far = Fetch(far_ref, [far_part_ref], (0, half), matrix, sems.at[1], yours)
        near.start()
        far.start()
        for c in range(2):

            @pl.when(core_ref[0] == c)
            def _():
                for g in range(groups):
                    at = slice(c * half + g * lanes, c * half + (g + 1) * lanes)
                    attended[:, at] = here_ref[g]
                    at = slice((1 - c) * half + g * lanes, (1 - c) * half + (g + 1) * lanes)
                    attended[:, at] = there_ref[g]

        near.wait()
        far.wait()
        for n in range(0, D, 256):
            branch[:, n : n + 256] = nn(attended[...], matrix[:, n : n + 256])
        bias, gain, shift = vector_ref[2:3], vector_ref[3:4], vector_ref[4:5]
        for at in row_blocks(rows):
            hidden = input_ref[at].astype(F32) + branch[at] + bias
            standardized, deviation = standardize(hidden)
            result = standardized * gain + shift
            normed[at] = result
            standard[at] = standardized
            inverse[at] = jnp.broadcast_to(deviation, (32, 128))
            low[at] = result.astype(BF)

    return block_call(
        kernel,
        "out_norm",
        [
            shaped((rows, D), F32),
            shaped((rows, D), F32),
            shaped((rows, 128), F32),
            shaped((rows, D)),
            shaped((rows, D)),
            shaped((D, D)),
        ],
        [core, near_table, far_table],
        [here, there, inputs, vectors],
        [*near_parts, far_part],
        [pltpu.VMEM((rows, D), F32), pltpu.SemaphoreType.DMA((2, chips))],
        2 * rows * D * D,
    )


def feed_forward(table, back_table, low_own, low_other, bias, in_parts, back_parts):
    rows = low_own.shape[0]
    units = bias.shape[1]
    chips = table.shape[0]
    tile = 256

    def kernel(table_ref, back_ref, own_ref, other_ref, bias_ref, *refs):
        n = len(in_parts)
        parts, back, refs = refs[:n], refs[n : 2 * n], refs[2 * n :]
        fed_own, fed_other, active, slope, low, in_mat, back_here, sems = refs
        first = Fetch(table_ref, parts, (0, units), in_mat, sems.at[0])
        second = Fetch(back_ref, back, (0, D), back_here, sems.at[1])
        first.start()
        low[:rows] = own_ref[...]
        low[rows:] = other_ref[...]
        first.wait()
        second.start()
        for t in range(0, units, tile):
            at = slice(t, t + tile)
            inner = nn(low[...], in_mat[:, at]) + bias_ref[:, at]
            share = 0.5 + 0.5 * lax.erf(inner * (0.5**0.5))
            active[:, at] = (inner * share).astype(BF)
            bell = jnp.exp(inner * inner * -0.5) * (1.0 / (2.0 * np.pi) ** 0.5)
            slope[:, at] = (share + inner * bell).astype(BF)
        second.wait()
        for n in range(0, D, tile):
            at = slice(n, n + tile)
            fed = nn(active[...], back_here[:, at])
            fed_own[:, at] = fed[:rows]
            fed_other[:, at] = fed[rows:].astype(BF)

    return block_call(
        kernel,
        "feed_forward",
        [
            shaped((rows, D), F32),
            shaped((rows, D)),
            shaped((2 * rows, units)),
            shaped((2 * rows, units)),
        ],
        [table, back_table],
        [low_own, low_other, bias],
        [*in_parts, *back_parts],
        [
            pltpu.VMEM((2 * rows, D), BF),
            pltpu.VMEM((D, units), BF),
            pltpu.VMEM((units, D), BF),
            pltpu.SemaphoreType.DMA((2, chips)),
        ],
        8 * rows * D * units,
    )


def last_norm(normed, fed_own, fed_there, vectors, cotangent):
    rows = normed.shape[0]

    def kernel(normed_ref, own_ref, there_ref, vector_ref, up_ref, result, grad, low, sums):
        bias, gain, shift = vector_ref[5:6], vector_ref[6:7], vector_ref[7:8]
        totals = [jnp.zeros((8, D), F32) for _ in range(3)]
        for at in row_blocks(rows):
            hidden = normed_ref[at] + own_ref[at] + there_ref[at].astype(F32) + bias
            standardized, deviation = standardize(hidden)
            result[at] = (standardized * gain + shift).astype(BF)
            up = up_ref[at].astype(F32)
            down = norm_backward(up, standardized, deviation, gain)
            grad[at] = down
            down_low = down.astype(BF)
            low[at] = down_low
            for n, term in enumerate((up * standardized, up, down_low.astype(F32))):
                totals[n] = totals[n] + fold(term, jnp.add)
        sums[...] = jnp.concatenate(
            [jnp.sum(total, 0, keepdims=True) for total in totals] + [jnp.zeros((5, D), F32)],
            axis=0,
        )

    return block_call(
        kernel,
        "last_norm",
        [shaped((rows, D)), shaped((rows, D), F32), shaped((rows, D)), shaped((8, D), F32)],
        [],
        [normed, fed_own, fed_there, vectors, cotangent],
        [],
        [],
        64 * rows * D,
    )


def place_pieces(value, first, rows, table_ref, stack, columns, at_row=0):
    for q in range(value.shape[0] // rows):
        piece = value[q * rows : (q + 1) * rows].astype(BF)
        stack[table_ref[first + q], at_row : at_row + rows, columns] = piece


def split_pieces(stack, keep, away, sems):
    half = keep.shape[0]
    copies = [
        pltpu.make_async_copy(stack.at[pl.ds(n * half, half)], out, sems.at[n])
        for n, out in enumerate((keep, away))
    ]
    for copy in copies:
        copy.start()
    for copy in copies:
        copy.wait()


def pieces_scratch(count, rows, columns):
    return [pltpu.VMEM((count, rows, columns), BF), pltpu.SemaphoreType.DMA((2,))]


def grad_back(table, active, up_own, up_other):
    rows = up_own.shape[0]
    units = active.shape[1]
    chips = table.shape[0]
    part = units // chips
    tile = 256

    def kernel(table_ref, active_ref, own_ref, other_ref, keep, away, stack, sems, up):
        up[:rows] = own_ref[...]
        up[rows:] = other_ref[...]
        for t in range(0, units, tile):
            value = tn(active_ref[:, t : t + tile], up[...])
            place_pieces(value, t // part, part, table_ref, stack, slice(0, D))
        split_pieces(stack, keep, away, sems)

    return block_call(
        kernel,
        "grad_back",
        [shaped((chips // 2, part, D))] * 2,
        [table],
        [active, up_own, up_other],
        [],
        [*pieces_scratch(chips, part, D), pltpu.VMEM((2 * rows, D), BF)],
        4 * rows * units * D,
        pl.ANY,
    )


def feed_backward(table, back_table, up_own, up_other, slope, in_parts, back_parts):
    rows = up_own.shape[0]
    units = slope.shape[1]
    chips = table.shape[0]
    tile = 256

    def kernel(table_ref, back_ref, own_ref, other_ref, slope_ref, *refs):
        n = len(in_parts)
        parts, back, refs = refs[:n], refs[n : 2 * n], refs[2 * n :]
        down_own, down_other, grad_inner, bias, up, in_mat, back_here, sems = refs
        first = Fetch(table_ref, parts, (0, units), in_mat, sems.at[0])
        second = Fetch(back_ref, back, (0, D), back_here, sems.at[1])
        second.start()
        up[:rows] = own_ref[...]
        up[rows:] = other_ref[...]
        second.wait()
        first.start()
        for t in range(0, units, tile):
            at = slice(t, t + tile)
            inner = (nt(up[...], back_here[at]) * slope_ref[:, at].astype(F32)).astype(BF)
            grad_inner[:, at] = inner
            bias[:, at] = jnp.sum(fold(inner.astype(F32), jnp.add), 0, keepdims=True)
        first.wait()
        for n in range(0, D, tile):
            at = slice(n, n + tile)
            down = nt(grad_inner[...], in_mat[at])
            down_own[:, at] = down[:rows]
            down_other[:, at] = down[rows:].astype(BF)

    return block_call(
        kernel,
        "feed_backward",
        [
            shaped((rows, D), F32),
            shaped((rows, D)),
            shaped((2 * rows, units)),
            shaped((1, units), F32),
        ],
        [table, back_table],
        [up_own, up_other, slope],
        [*in_parts, *back_parts],
        [
            pltpu.VMEM((2 * rows, D), BF),
            pltpu.VMEM((D, units), BF),
            pltpu.VMEM((units, D), BF),
            pltpu.SemaphoreType.DMA((2, chips)),
        ],
        8 * rows * D * units,
    )


def out_norm_backward(
    core, grad_two, down_own, down_there, standard, inverse, vectors, attended, matrix
):
    rows = grad_two.shape[0]
    half = D // 2
    lanes = 128 if half % 128 == 0 else half

    def kernel(
        core_ref,
        two_ref,
        own_ref,
        there_ref,
        standard_ref,
        inverse_ref,
        vector_ref,
        attended_ref,
        matrix_ref,
        grad_one,
        low,
        sums,
        grad_heads,
        grad_far,
    ):
        gain = vector_ref[3:4]
        totals = [jnp.zeros((8, D), F32) for _ in range(3)]
        for at in row_blocks(rows):
            grad = two_ref[at] + own_ref[at] + there_ref[at].astype(F32)
            standardized = standard_ref[at]
            down = norm_backward(grad, standardized, inverse_ref[at, :1], gain)
            grad_one[at] = down
            down_low = down.astype(BF)
            low[at] = down_low
            for n, term in enumerate((grad * standardized, grad, down_low.astype(F32))):
                totals[n] = totals[n] + fold(term, jnp.add)
        sums[...] = jnp.concatenate(
            [jnp.sum(total, 0, keepdims=True) for total in totals] + [jnp.zeros((5, D), F32)],
            axis=0,
        )
        for n in range(0, D, 256):
            grad_heads[:, n : n + 256] = nt(low[...], matrix_ref[n : n + 256]).astype(BF)
        yours = pl.ds(pl.multiple_of((1 - core_ref[0]) * half, half), half)
        for n in range(0, D, 256):
            grad_far[n : n + 256] = tn(attended_ref[:, n : n + 256], low[:, yours]).astype(BF)

    return block_call(
        kernel,
        "out_norm_backward",
        [
            shaped((rows, D), F32),
            shaped((rows, D)),
            shaped((8, D), F32),
            shaped((rows, D)),
            shaped((D, half)),
        ],
        [core],
        [grad_two, down_own, down_there, standard, inverse, vectors, attended, matrix],
        [],
        [],
        3 * rows * D * D,
    )


def grad_in_out(core, table, low_own, low_other, grad_inner, attended, low_grad, far):
    rows = low_own.shape[0]
    units = grad_inner.shape[1]
    chips = table.shape[0]
    shard = D // chips
    half = D // 2
    tile = 256

    def kernel(
        core_ref,
        table_ref,
        own_ref,
        other_ref,
        inner_ref,
        attended_ref,
        grad_ref,
        far_ref,
        keep,
        away,
        stack,
        sems,
        low,
    ):
        low[:rows] = own_ref[...]
        low[rows:] = other_ref[...]
        mine = pl.ds(pl.multiple_of(core_ref[0] * half, half), half)
        for t in range(0, D, tile):
            at = slice(t, t + tile)
            value = tn(low[:, at], inner_ref[...])
            place_pieces(value, t // shard, shard, table_ref, stack, slice(0, units))
            value = tn(attended_ref[:, at], grad_ref[:, mine]) + far_ref[at].astype(F32)
            place_pieces(value, t // shard, shard, table_ref, stack, slice(units, units + half))
        split_pieces(stack, keep, away, sems)

    return block_call(
        kernel,
        "grad_in_out",
        [shaped((chips // 2, shard, units + half))] * 2,
        [core, table],
        [low_own, low_other, grad_inner, attended, low_grad, far],
        [],
        [*pieces_scratch(chips, shard, units + half), pltpu.VMEM((2 * rows, D), BF)],
        5 * rows * units * D,
        pl.ANY,
    )


def grad_projections(
    numbers, table, tokens_own, tokens_other, down_own, down_other, sums_one, sums_two, in_bias, extra
):
    half, rows, width = down_own.shape
    lanes = width // 3
    chips = table.shape[0]
    shard = D // chips
    units = in_bias.shape[1]
    part = units // chips
    tile = 256

    def kernel(
        number_ref,
        table_ref,
        x_own,
        x_other,
        own_ref,
        other_ref,
        one_ref,
        two_ref,
        bias_ref,
        keep,
        away,
        stack,
        sems,
    ):
        own = own_ref[...].reshape(half * rows, width)
        other = other_ref[...].reshape(half * rows, width)
        for t in range(0, D, tile):
            value = jnp.zeros((tile, width), F32)
            for p in range(half):
                value = value + tn(x_own[p, :, t : t + tile], own_ref[p])
                value = value + tn(x_other[p, :, t : t + tile], other_ref[p])
            place_pieces(value, t // shard, shard, table_ref, stack, slice(0, width))
        totals = jnp.sum(
            fold(own.astype(F32), jnp.add) + fold(other.astype(F32), jnp.add),
            0,
            keepdims=True,
        )
        pair = jnp.concatenate([totals[:, :lanes], totals[:, 2 * lanes :]], axis=0)
        pair = jnp.concatenate(
            [jnp.where(number_ref[1] == a, pair, 0.0) for a in range(D // lanes)], axis=1
        )
        one, two = one_ref[...], two_ref[...]
        stacked = jnp.concatenate(
            [pair, one[2:3], one[0:1], one[1:2], two[2:3], two[0:1], two[1:2]], axis=0
        )
        blank = jnp.zeros((1, part), F32)
        for i in range(chips):
            bias = bias_ref[:, i * part : (i + 1) * part]
            bias = jnp.where(
                number_ref[0] == 0,
                jnp.concatenate([bias, blank], axis=1),
                jnp.concatenate([blank, bias], axis=1),
            )
            top = stacked[:, i * shard : (i + 1) * shard]
            rest = extra - 9
            block = jnp.concatenate(
                [
                    jnp.concatenate([top, jnp.zeros((8, width - shard), F32)], axis=1),
                    jnp.concatenate([bias, jnp.zeros((1, width - 2 * part), F32)], axis=1),
                    jnp.zeros((rest, width), F32),
                ],
                axis=0,
            )
            place_pieces(block, i, extra, table_ref, stack, slice(0, width), shard)
        split_pieces(stack, keep, away, sems)

    return block_call(
        kernel,
        "grad_projections",
        [shaped((chips // 2, shard + extra, width))] * 2,
        [numbers, table],
        [
            tokens_own,
            tokens_other,
            down_own,
            down_other,
            sums_one,
            sums_two,
            in_bias,
        ],
        [],
        pieces_scratch(chips, shard + extra, width),
        4 * half * rows * D * width,
        pl.ANY,
    )


def pack(numbers, weights, vectors, bias, marks, groups, extra):
    shard = weights[0].shape[0]
    half = D // 2
    lanes = half // groups
    width = 3 * lanes

    def kernel(number_ref, *refs):
        *weight_refs, vector_ref, bias_ref, mark_ref, out = refs

        def lines(row):
            count = -(-row.shape[1] // width)
            padded = jnp.concatenate(
                [row, jnp.zeros((1, count * width - row.shape[1]), F32)], axis=1
            )
            return [padded[:, n * width : (n + 1) * width] for n in range(count)]

        small = vector_ref[...].astype(F32)
        block = [jnp.concatenate([small, jnp.zeros((8, width - small.shape[1]), F32)], axis=1)]
        block += lines(bias_ref[...].astype(F32)) + lines(mark_ref[...].astype(F32))
        filled = 8 + len(block) - 1
        block = jnp.concatenate(block + [jnp.zeros((extra - filled, width), F32)], axis=0)
        block = block.astype(BF)
        for d in range(groups):
            out[d, shard:] = block
        for c in range(2):

            @pl.when(number_ref[0] == c)
            def _():
                for a in range(groups):
                    place = number_ref[2 + a]
                    for n, weight in enumerate(weight_refs):
                        start = c * half + a * lanes
                        out[place, :shard, n * lanes : (n + 1) * lanes] = weight[
                            :, start : start + lanes
                        ]

    return block_call(
        kernel,
        "pack",
        [shaped((groups, shard + extra, width))],
        [numbers],
        [*weights, vectors, bias, marks],
        [],
        [],
        0,
    )[0]


def send(value, perm):
    return lax.ppermute(value, AXES, perm)


def gather_stages(block, perms):
    for perm in perms[:-1]:
        block = jnp.concatenate([block, send(block, perm)], axis=0)
    return [block, send(block, perms[-1])]


def hold(value, *earlier):
    return lax.optimization_barrier((value, *earlier))[0]


class Gather:
    def __init__(self, block, perms):
        self.parts, self.perms = [block], perms

    def stage(self, *earlier):
        first = hold(self.parts[0], *earlier) if earlier else self.parts[0]
        block = jnp.concatenate([first, *self.parts[1:]], axis=0)
        self.parts = [block, send(block, self.perms[0])]
        self.perms = self.perms[1:]
        return self.parts[1]


class Scatter:
    def __init__(self, keep, away, perms):
        self.keep, self.away, self.perms = keep, away, perms[::-1]

    def stage(self, *earlier):
        arrived = send(self.away, self.perms[0])
        arrived = hold(arrived, *earlier) if earlier else arrived
        self.perms = self.perms[1:]
        if self.perms:
            half = self.keep.shape[0] // 2
            self.away = self.keep[half:] + arrived[half:]
            self.keep = self.keep[:half] + arrived[:half]
        else:
            self.keep = self.keep.astype(F32) + arrived.astype(F32)
        return arrived

    def finish(self):
        while self.perms:
            self.stage()
        return self.keep


def pieces(count, rows, columns):
    return jax.ShapeDtypeStruct((count, rows, columns), BF)


def body(
    plan,
    tokens,
    segment_ids,
    w_query,
    b_query,
    w_key,
    w_value,
    b_value,
    w_out,
    b_out,
    g_attn,
    n_attn,
    w_in,
    b_in,
    w_back,
    b_back,
    g_ffn,
    n_ffn,
    cotangent,
):
    chips, groups, heads, ctx = plan.chips, plan.groups, plan.heads, plan.ctx
    core = lax.axis_index("dp")
    place = lax.axis_index("ctx")
    device = (core * ctx + place) * plan.fsdp + lax.axis_index("fsdp")
    side, group = place // groups, place % groups
    rows = tokens.shape[1]
    shard = w_query.shape[0]
    hidden = w_back.shape[0]
    part = hidden // 2
    units = FF // 2
    lanes = heads * HD
    half_d = D // 2
    width = 3 * lanes
    bias_rows, mark_rows = -(-hidden // width), -(-rows // width)
    extra = 16 * (-(-(8 + bias_rows + mark_rows) // 16))
    swap = plan.core_swap()
    in_perms = plan.chip_perms(plan.in_orders)
    back_perms = plan.chip_perms(plan.back_orders)

    side_table = plan.side_pieces()
    tables = dict(
        w_in=plan.chip_gather(plan.in_orders),
        far=plan.other_core(plan.chip_gather(plan.in_orders)),
        w_back=plan.chip_gather(plan.back_orders),
        pieces=invert(side_table),
        chunks=plan.table(lambda c, j, f: [plan.chunk_of(c, j, p) for p in range(ctx)]),
        numbers=plan.table(
            lambda c, j, f: [c, c * groups + j % groups]
            + [a ^ (j % groups) for a in range(groups)]
        ),
    )
    table_row = lax.dynamic_index_in_dim(
        jnp.asarray(np.concatenate(list(tables.values()), axis=1)), device, 0, False
    )
    starts = np.cumsum([0] + [t.shape[1] for t in tables.values()])
    look = {
        name: table_row[starts[n] : starts[n + 1]] for n, name in enumerate(tables)
    }

    def mine(columns, size, axis=1):
        return lax.dynamic_slice_in_dim(columns, core * size, size, axis)

    w_in_mine = lax.dynamic_index_in_dim(
        w_in.reshape(shard, chips, 2, part), core, 2, False
    ).reshape(shard, units)
    w_in_mine = jnp.concatenate([w_in_mine, mine(w_out, half_d)], axis=1)[None]
    w_back_mine = mine(w_back, part, 0)[None]
    in_gather = Gather(w_in_mine, in_perms)
    back_gather = Gather(w_back_mine, back_perms)

    inputs = tokens[0]
    turned = send(inputs, plan.turn())
    block = turned[None]
    reached = [turned]
    for perm in plan.group_perms():
        reached.append(send(block, perm))
        block = jnp.concatenate([block, reached[-1]], axis=0)
    tokens_own = block
    tokens_other = send(tokens_own, swap)
    in_gather.stage(turned)
    in_gather.stage(reached[1])
    back_gather.stage(reached[1])
    in_gather.stage(reached[2])
    back_gather.stage(reached[2])

    vectors = jnp.stack([b_query, b_value, b_out, g_attn, n_attn, b_back, g_ffn, n_ffn])
    messages = pack(
        look["numbers"],
        [w_query, w_key, w_value],
        vectors,
        b_in[None],
        segment_ids,
        groups,
        extra,
    )
    arrived = [messages[0]] + [
        send(messages[d], plan.group_direct(d)) for d in range(1, groups)
    ]
    gathered = gather_stages(hold(jnp.stack(arrived), reached[1]), plan.side_perms())
    heads_mat, extras = route(
        gathered,
        look["pieces"],
        [pieces(chips, shard, width), pieces(chips, extra, width)],
        [((0, 1), i, 0, shard, 0, i, 0) for i in range(chips)]
        + [((0, 1), i, shard, extra, 1, i, 0) for i in range(chips)],
    )
    heads_mat = heads_mat.reshape(D, width)
    vectors = extras[:, :8, :shard].transpose(1, 0, 2).reshape(8, D).astype(F32)
    in_bias = extras[:, 8 : 8 + bias_rows].reshape(chips, -1)[:, :hidden]
    in_bias = (
        lax.dynamic_slice_in_dim(in_bias, core * part, part, 1).reshape(1, units).astype(F32)
    )
    at = 8 + bias_rows
    ids_here = extras[:, at : at + mark_rows].reshape(chips, -1)[:, :rows]
    ids_here = lax.dynamic_index_in_dim(
        ids_here.reshape(ctx, plan.fsdp, rows), lax.axis_index("fsdp"), 1, False
    )
    ids_there = send(ids_here, swap)
    ids_all = jnp.where(core == side, ids_here, ids_there).astype(F32)
    chosen = look["chunks"][:, None] == jnp.arange(ctx)[None]
    ids = jnp.sum(jnp.where(chosen[:, :, None], ids_all[None], 0.0), axis=1)
    first, last = ids[:, 0], ids[:, -1]
    overlap = ((first[:, None] <= last[None]) & (first[None] <= last[:, None])).astype(jnp.int32)
    ids = ids[:, None, :]
    meets = listing(overlap)

    start = core * half_d + group * lanes
    heads_bias = jnp.concatenate(
        [
            lax.dynamic_slice(vectors, (0, start), (1, lanes)),
            jnp.zeros((1, lanes), F32),
            lax.dynamic_slice(vectors, (1, start), (1, lanes)),
        ],
        axis=1,
    )

    def project(block):
        return (
            jnp.einsum("ptd,dw->ptw", block, heads_mat, preferred_element_type=F32) + heads_bias
        ).astype(BF)

    qkv_own, qkv_other = project(tokens_own), project(tokens_other)
    in_gather.stage(qkv_own)
    in_parts = in_gather.parts
    back_gather.stage(qkv_own)
    qkv_other = hold(qkv_other, in_parts[0], back_gather.parts[0])
    sent, flat, totals = attend_forward(
        look["chunks"], qkv_own, qkv_other, ids, meets, heads
    )
    met = lax.all_to_all(sent, "ctx", 0, 0, tiled=True).reshape(2, groups, rows, lanes)
    back_gather.stage(met, in_parts[1])
    back_parts = back_gather.parts
    out_there = jnp.concatenate([part[:, :, units:] for part in in_parts], axis=0)
    out_there = send(out_there, swap)
    here = lax.dynamic_index_in_dim(met, core, 0, False)
    there = send(lax.dynamic_index_in_dim(met, 1 - core, 0, False), swap)

    core_number = look["numbers"][:1]
    normed, standard, inverse, low_own, attended, out_mat = out_norm(
        core_number,
        look["w_in"],
        look["far"],
        here,
        there,
        inputs,
        vectors,
        in_parts,
        out_there,
        units,
    )
    low_other = send(low_own, swap)
    fed_own, fed_other, active, slope = feed_forward(
        look["w_in"], look["w_back"], low_own, low_other, in_bias, in_parts, back_parts
    )
    result, grad_two, up_own, sums_two = last_norm(
        normed, fed_own, send(fed_other, swap), vectors, cotangent[0]
    )
    up_other = send(up_own, swap)
    down_own, down_other, grad_inner, grad_in_bias = feed_backward(
        look["w_in"],
        look["w_back"],
        up_own,
        up_other,
        slope,
        in_parts,
        back_parts,
    )
    grad_one, low_grad, sums_one, grad_heads, grad_far = out_norm_backward(
        core_number,
        grad_two,
        down_own,
        send(down_other, swap),
        standard,
        inverse,
        vectors,
        attended,
        out_mat,
    )
    grad_heads = grad_heads.reshape(rows, 2, groups, lanes).transpose(1, 2, 0, 3)
    kept = lax.dynamic_index_in_dim(grad_heads, core, 0, False)
    towards = send(lax.dynamic_index_in_dim(grad_heads, 1 - core, 0, False), swap)
    grad_heads = jnp.where(
        core == 0, jnp.stack([kept, towards]), jnp.stack([towards, kept])
    ).reshape(ctx, rows, lanes)
    grads = lax.all_to_all(grad_heads, "ctx", 0, 0, tiled=True)
    back_scatter = Scatter(
        *grad_back(look["w_back"], hold(active, grad_heads), up_own, up_other), back_perms
    )
    in_scatter = Scatter(
        *grad_in_out(
            core_number,
            look["w_in"],
            low_own,
            low_other,
            hold(grad_inner, back_scatter.away),
            attended,
            low_grad,
            send(grad_far, swap),
        ),
        in_perms,
    )

    grads = hold(grads, in_scatter.away)
    back_first = back_scatter.stage()
    in_first = in_scatter.stage()
    qkv_grads = attend_backward(
        look["chunks"], qkv_own, qkv_other, ids, meets, grads, flat, totals, heads
    )
    qkv_grads = lax.optimization_barrier((*qkv_grads, back_first))[:2]
    down_own, down_other = qkv_grads

    def back_project(down):
        return jnp.einsum("ptw,dw->ptd", down, heads_mat, preferred_element_type=F32)

    towards = send(back_project(down_other).astype(BF), swap)
    block = (back_project(down_own) + towards.astype(F32)).astype(BF)
    whole_block = block
    down_own, down_other, _ = lax.optimization_barrier((down_own, down_other, block))
    side_scatter = Scatter(
        *grad_projections(
            look["numbers"],
            look["pieces"],
            tokens_own,
            tokens_other,
            down_own,
            down_other,
            sums_one,
            sums_two,
            grad_in_bias,
            extra,
        ),
        plan.side_perms(),
    )
    reached = []
    for perm in plan.group_perms()[::-1]:
        half = block.shape[0] // 2
        reached.append(send(block[half:], perm))
        block = block[:half] + reached[-1]
    in_scatter.stage(whole_block)
    back_scatter.stage(whole_block)
    in_scatter.stage(reached[0])
    side_scatter.stage(reached[0])
    in_away = in_scatter.away
    back_scatter.stage(reached[1])
    ended = send(hold(block[0], in_away), plan.turn())
    side_last = send(side_scatter.away, side_scatter.perms[0])
    low_by_group = (side_scatter.keep + hold(side_last, reached[1]))
    back_last = back_scatter.finish()
    grad_back_mat = hold(back_last[0], reached[1])
    grad_inputs = grad_one + ended.astype(F32)
    in_last = in_scatter.finish()
    in_scatter.keep = hold(in_last, reached[1])
    by_group = [low_by_group[0]] + [
        send(low_by_group[d], plan.group_direct(d)) for d in range(1, groups)
    ]
    by_group = jnp.stack(by_group).astype(F32)
    grad_extras = jnp.sum(by_group[:, shard:], 0)
    grad_columns = jnp.stack(
        [lax.dynamic_index_in_dim(by_group, group ^ d, 0, False)[:shard] for d in range(groups)]
    )
    grad_columns = grad_columns.reshape(groups, shard, 3, lanes).transpose(2, 1, 0, 3)
    grad_columns = grad_columns.reshape(3, shard, half_d)
    grad_in_mat = in_scatter.finish()[0]
    grad_out_mat = grad_in_mat[:, units:]
    grad_in_mat = grad_in_mat[:, :units]

    def both(half, axis):
        there = send(half, swap)
        return jnp.where(
            core == 0, jnp.stack([half, there], axis=axis), jnp.stack([there, half], axis=axis)
        )

    grad_columns = both(grad_columns, 2).reshape(3, shard, D)
    grad_out_mat = both(grad_out_mat, 1).reshape(shard, D)
    grad_in_mat = both(grad_in_mat.reshape(shard, chips, part), 2).reshape(
        shard, FF
    )
    grad_back_mat = both(grad_back_mat, 0).reshape(hidden, D)
    sums = grad_extras + send(grad_extras, swap)
    small = [sums[which, :shard] for which in range(8)]
    return (
        result[None],
        grad_inputs[None],
        grad_columns[0],
        small[0],
        grad_columns[1],
        grad_columns[2],
        small[1],
        grad_out_mat,
        small[2],
        small[3],
        small[4],
        grad_in_mat,
        sums[8:].reshape(-1)[:hidden],
        grad_back_mat,
        small[5],
        small[6],
        small[7],
    )


def solution(mesh):
    owned = ("ctx", "fsdp")
    matrix, vector = P(owned, None), P(owned)
    sequence = P(("dp", "fsdp"), "ctx", None)
    return jax.shard_map(
        partial(body, Plan(mesh)),
        mesh=mesh,
        in_specs=(
            sequence,
            P(("dp", "fsdp"), "ctx"),
            matrix,
            vector,
            matrix,
            matrix,
            vector,
            matrix,
            vector,
            vector,
            vector,
            matrix,
            vector,
            matrix,
            vector,
            vector,
            vector,
            sequence,
        ),
        out_specs=(
            sequence,
            sequence,
            matrix,
            vector,
            matrix,
            matrix,
            vector,
            matrix,
            vector,
            vector,
            vector,
            matrix,
            vector,
            matrix,
            vector,
            vector,
            vector,
        ),
        check_vma=False,
    )
```

```python
from functools import partial

import jax
import jax.numpy as jnp
import numpy as np
from jax import lax
from jax.experimental import pallas as pl
from jax.experimental.pallas import tpu as pltpu
from jax.sharding import PartitionSpec as P

D = 1024
H = 16
HD = 64
FF = 4096
NORM_EPS = 1e-05
NEG_FILL = -1e30
AXES = ("dp", "ctx", "fsdp")
BF = jnp.bfloat16
F32 = jnp.float32
VMEM_LIMIT = 48 * 1024 * 1024


def subset_masks(order):
    table = [0]
    for mask in order:
        table = table + [mask ^ entry for entry in table]
    return table


def bits_of(count):
    return [1 << t for t in range(count.bit_length() - 1)]


class Plan:
    def __init__(self, mesh):
        self.ctx = mesh.shape["ctx"]
        self.fsdp = mesh.shape["fsdp"]
        self.chips = self.ctx * self.fsdp
        self.groups = self.ctx // 2
        self.heads = H // self.ctx
        self.devices = [
            (c, j, f) for c in range(2) for j in range(self.ctx) for f in range(self.fsdp)
        ]
        bits = bits_of(self.chips)
        self.in_orders = [bits[:1:-1] + [1, 2], bits[:1:-1] + [2, 1]]
        self.back_orders = self.in_orders
        group_bits = bits_of(self.groups)
        self.group_orders = [group_bits[::-1], group_bits]
        self.group_masks = [subset_masks(order) for order in self.group_orders]
        top = self.groups * self.fsdp
        self.side_orders = [[top] + bits_of(self.fsdp)] * 2
        self.side_masks = [subset_masks(order) for order in self.side_orders]

    def flat(self, c, j, f):
        return (c * self.ctx + j) * self.fsdp + f

    def perm(self, move):
        return [(self.flat(*dev), self.flat(*move(*dev))) for dev in self.devices]

    def chip_xor(self, masks):
        def move(c, j, f):
            i = (j * self.fsdp + f) ^ masks[c]
            return (c, i // self.fsdp, i % self.fsdp)

        return self.perm(move)

    def chip_perms(self, orders):
        return [self.chip_xor(pair) for pair in zip(*orders)]

    def side_perms(self):
        return [self.chip_xor(pair) for pair in zip(*self.side_orders)]

    def group_perms(self):
        return [
            self.perm(lambda c, j, f, pair=pair: (c, j ^ pair[c], f))
            for pair in zip(*self.group_orders)
        ]

    def group_direct(self, d):
        return self.perm(lambda c, j, f: (c, j ^ d, f))

    def core_swap(self):
        return self.perm(lambda c, j, f: (1 - c, j, f))

    def turn(self):
        def move(c, j, f):
            return (j // self.groups, c * self.groups + j % self.groups, f)

        return self.perm(move)

    def chunk_of(self, c, j, p):
        e, k = divmod(p, self.groups)
        return (c ^ e) * self.groups + ((j % self.groups) ^ self.group_masks[c ^ e][k])

    def table(self, entries):
        return np.array([entries(*dev) for dev in self.devices], np.int32)

    def chip_gather(self, orders):
        def entries(c, j, f):
            inverse = np.argsort(subset_masks(orders[c]))
            return [inverse[(j * self.fsdp + f) ^ i] for i in range(self.chips)]

        return self.table(entries)

    def other_core(self, table):
        return table.reshape(2, -1, table.shape[1])[::-1].reshape(table.shape)

    def side_pieces(self):
        def entries(c, j, f):
            return [
                (j * self.fsdp + f) ^ mask ^ (d * self.fsdp)
                for mask in self.side_masks[c]
                for d in range(self.groups)
            ]

        return self.table(entries)


def invert(table):
    return np.argsort(table, axis=1).astype(np.int32)


def route(sources, table, outs, moves):
    def kernel(table_ref, *refs):
        ins, results, sems = refs[: len(sources)], refs[len(sources) : -1], refs[-1]

        def copy(m, source, piece):
            _, _, row, rows, out, out_piece, out_row = moves[m]
            return pltpu.make_async_copy(
                source.at[piece, pl.ds(row, rows)],
                results[out].at[out_piece, pl.ds(out_row, rows)],
                sems.at[m],
            )

        for m, (group, slot, *_) in enumerate(moves):
            index = table_ref[slot]
            start = 0
            for which in group:
                count = sources[which].shape[0]

                @pl.when((index >= start) & (index < start + count))
                def _():
                    copy(m, ins[which], index - start).start()

                start += count
        for m, (group, *_) in enumerate(moves):
            copy(m, ins[group[0]], 0).wait()

    total = sum(
        moves[m][3] * outs[moves[m][4]].shape[2] * outs[moves[m][4]].dtype.itemsize
        for m in range(len(moves))
    )
    return pl.pallas_call(
        kernel,
        out_shape=outs,
        in_specs=[pl.BlockSpec(memory_space=pltpu.SMEM)]
        + [pl.BlockSpec(memory_space=pl.ANY)] * len(sources),
        out_specs=[pl.BlockSpec(memory_space=pltpu.VMEM)] * len(outs),
        scratch_shapes=[pltpu.SemaphoreType.DMA((len(moves),))],
        compiler_params=pltpu.CompilerParams(vmem_limit_bytes=VMEM_LIMIT),
        cost_estimate=pl.CostEstimate(flops=0, bytes_accessed=0, transcendentals=0),
    )(table, *sources)


def nt(left, right):
    return lax.dot_general(left, right, (((1,), (1,)), ((), ())), preferred_element_type=F32)


def nn(left, right):
    return lax.dot_general(left, right, (((1,), (0,)), ((), ())), preferred_element_type=F32)


def tn(left, right):
    return lax.dot_general(left, right, (((0,), (0,)), ((), ())), preferred_element_type=F32)


def column_ids(row):
    return jnp.transpose(jnp.broadcast_to(row, (128, row.shape[1])))


def listing(overlap):
    count = overlap.shape[0]
    before = jnp.arange(count)[None, :] < jnp.arange(count)[:, None]
    rank = jnp.sum(jnp.where(before[None], overlap[:, None, :], 0), 2)
    slot = jnp.where(overlap > 0, rank, count)
    here = slot[:, None, :] == jnp.arange(count)[None, :, None]
    order = jnp.sum(jnp.where(here, jnp.arange(count)[None, None, :], 0), 2)
    return jnp.concatenate([order, jnp.sum(overlap, 1, keepdims=True)], 1).astype(jnp.int32)


def fold(values, combine):
    rows = values.shape[0]
    while rows > 8:
        rows //= 2
        values = combine(values[:rows], values[rows:])
    return values


def looped(count, step, carry):
    pairs = count // 2
    carry = lax.fori_loop(0, pairs, lambda t, c: step(2 * t + 1, step(2 * t, c)), carry)
    return lax.fori_loop(2 * pairs, count, step, carry)


def same_document(columns, row):
    repeats = -(-columns.shape[0] // 128)
    return jnp.concatenate([columns] * repeats, axis=1)[:, : row.shape[1]] == row


def one_head(flat, h, heads):
    zero = jnp.zeros((HD, flat.shape[1]), flat.dtype)
    return jnp.concatenate(
        [flat[g * HD : (g + 1) * HD] if g == h else zero for g in range(heads)], axis=0
    )


def attend_forward(places, qkv_own, qkv_other, ids, meets, heads):
    half, rows, width = qkv_own.shape
    chunks = 2 * half
    lanes = heads * HD

    def kernel(list_ref, place_ref, own_ref, other_ref, ids_ref, *refs):
        out_ref, flat_ref, total_ref, keys, values, queries, cols, logits_ref = refs
        step = pl.program_id(0)

        @pl.when(step == 0)
        def _():
            for p in range(chunks):
                block = (own_ref if p < half else other_ref)[p % half]
                query = jnp.transpose(block[:, :lanes] * BF(HD**-0.5))
                for h in range(heads):
                    queries[p, h] = one_head(query, h, heads)
                keys[p] = block[:, lanes : 2 * lanes]
                values[p] = jnp.transpose(block[:, 2 * lanes :])
                cols[p] = column_ids(ids_ref[p])

        row_ids = ids_ref[step]
        count = list_ref[step, chunks]
        query = [queries[step, h] for h in range(heads)]

        def scores(t, highs):
            p = list_ref[step, t]
            same = same_document(cols[p], row_ids)
            key = keys[p]
            new = []
            for h in range(heads):
                logits = jnp.where(same, nn(key, query[h]), NEG_FILL)
                logits_ref[h, t] = logits
                new.append(jnp.maximum(highs[h], fold(logits, jnp.maximum)))
            return tuple(new)

        highs = looped(
            count, scores, tuple(jnp.full((8, rows), NEG_FILL, F32) for _ in range(heads))
        )
        highs = [jnp.max(high, 0, keepdims=True) for high in highs]

        def attend(t, sums):
            p = list_ref[step, t]
            new = []
            for h in range(heads):
                low, acc = sums[h]
                weights = jnp.exp(logits_ref[h, t] - highs[h])
                new.append(
                    (
                        low + fold(weights, jnp.add),
                        acc + nn(values[p, h * HD : (h + 1) * HD], weights.astype(BF)),
                    )
                )
            return tuple(new)

        sums = looped(
            count,
            attend,
            tuple(
                (jnp.zeros((8, rows), F32), jnp.zeros((HD, rows), F32)) for _ in range(heads)
            ),
        )
        lows = [jnp.sum(low, 0, keepdims=True) for low, _ in sums]
        flat = jnp.concatenate([acc / low for (_, acc), low in zip(sums, lows)], axis=0)
        flat_ref[0] = flat
        total_ref[0] = jnp.concatenate(
            [high + jnp.log(low) for high, low in zip(highs, lows)]
            + [jnp.zeros((8 - heads, rows), F32)],
            axis=0,
        )
        out_ref[0] = jnp.transpose(flat).astype(BF)

    whole = lambda *shape: pl.BlockSpec(shape, lambda i, o, q: (0,) * len(shape))
    pairs = chunks * chunks * heads
    return pl.pallas_call(
        kernel,
        name="attend_forward",
        out_shape=[
            jax.ShapeDtypeStruct((chunks, rows, lanes), BF),
            jax.ShapeDtypeStruct((chunks, lanes, rows), F32),
            jax.ShapeDtypeStruct((chunks, 8, rows), F32),
        ],
        grid_spec=pltpu.PrefetchScalarGridSpec(
            num_scalar_prefetch=2,
            grid=(chunks,),
            in_specs=[
                whole(half, rows, width),
                whole(half, rows, width),
                whole(chunks, 1, rows),
            ],
            out_specs=[
                pl.BlockSpec((1, rows, lanes), lambda i, o, q: (q[i], 0, 0)),
                pl.BlockSpec((1, lanes, rows), lambda i, o, q: (i, 0, 0)),
                pl.BlockSpec((1, 8, rows), lambda i, o, q: (i, 0, 0)),
            ],
            scratch_shapes=[
                pltpu.VMEM((chunks, rows, lanes), BF),
                pltpu.VMEM((chunks, lanes, rows), BF),
                pltpu.VMEM((chunks, heads, lanes, rows), BF),
                pltpu.VMEM((chunks, rows, 128), F32),
                pltpu.VMEM((heads, chunks, rows, rows), F32),
            ],
        ),
        compiler_params=pltpu.CompilerParams(vmem_limit_bytes=VMEM_LIMIT),
        cost_estimate=pl.CostEstimate(
            flops=pairs * rows * rows * 24000,
            bytes_accessed=chunks * rows * width * 4,
            transcendentals=pairs * rows * rows,
        ),
    )(meets, places, qkv_own, qkv_other, ids)


def attend_backward(places, qkv_own, qkv_other, ids, meets, grads, flat, totals, heads):
    half, rows, width = qkv_own.shape
    chunks = 2 * half
    lanes = heads * HD

    def kernel(
        list_ref, place_ref, own_ref, other_ref, ids_ref, flat_ref, total_ref, up_ref, *refs
    ):
        down_own, down_other = refs[:2]
        keys, turned, values, queries, cols, grad_key, grad_value = refs[2:]
        step = pl.program_id(0)

        @pl.when(step == 0)
        def _():
            for p in range(chunks):
                block = (own_ref if p < half else other_ref)[p % half]
                queries[p] = block[:, :lanes] * BF(HD**-0.5)
                keys[p] = block[:, lanes : 2 * lanes]
                turned[p] = jnp.transpose(block[:, lanes : 2 * lanes])
                values[p] = block[:, 2 * lanes :]
                cols[p] = column_ids(ids_ref[p])
            grad_key[...] = jnp.zeros_like(grad_key)
            grad_value[...] = jnp.zeros_like(grad_value)

        query = queries[step]
        up = up_ref[0]
        row_ids = ids_ref[step]
        count = list_ref[step, chunks]
        query_turned, up_turned = jnp.transpose(query), jnp.transpose(up)
        product = up_turned.astype(F32) * flat_ref[0]
        deltas = [
            jnp.sum(product[h * HD : (h + 1) * HD], 0, keepdims=True) for h in range(heads)
        ]
        total = total_ref[0]
        lane_head = lax.broadcasted_iota(jnp.int32, (rows, lanes), 1) // HD
        queries_turned = [one_head(query_turned, h, heads) for h in range(heads)]
        ups_turned = [one_head(up_turned, h, heads) for h in range(heads)]
        queries_wide = [jnp.where(lane_head == h, query, BF(0)) for h in range(heads)]
        ups_wide = [jnp.where(lane_head == h, up, BF(0)) for h in range(heads)]

        def one(t, carry):
            p = list_ref[step, t]
            same = same_document(cols[p], row_ids)
            key, value = keys[p], values[p]
            sum_key, sum_value = grad_key[p], grad_value[p]
            new = []
            for h in range(heads):
                logits = jnp.where(same, nn(key, queries_turned[h]), NEG_FILL)
                weights = jnp.exp(logits - total[h : h + 1])
                grad_prob = nn(value, ups_turned[h])
                grad_score = (weights * (grad_prob - deltas[h])).astype(BF)
                sum_value = sum_value + nn(weights.astype(BF), ups_wide[h])
                sum_key = sum_key + nn(grad_score, queries_wide[h])
                new.append(carry[h] + nn(turned[p, h * HD : (h + 1) * HD], grad_score))
            grad_value[p] = sum_value
            grad_key[p] = sum_key
            return tuple(new)

        acc = looped(count, one, tuple(jnp.zeros((HD, rows), F32) for _ in range(heads)))
        grad_query = (jnp.transpose(jnp.concatenate(acc, 0)) * HD**-0.5).astype(BF)
        for p in range(chunks):
            out = down_own if p < half else down_other

            @pl.when(step == p)
            def _():
                out[p % half, :, :lanes] = grad_query

            @pl.when(step == chunks - 1)
            def _():
                out[p % half, :, lanes : 2 * lanes] = grad_key[p].astype(BF)
                out[p % half, :, 2 * lanes :] = grad_value[p].astype(BF)

    whole = lambda *shape: pl.BlockSpec(shape, lambda i, o, q: (0,) * len(shape))
    pairs = chunks * chunks * heads
    return pl.pallas_call(
        kernel,
        name="attend_backward",
        out_shape=[jax.ShapeDtypeStruct((half, rows, width), BF)] * 2,
        grid_spec=pltpu.PrefetchScalarGridSpec(
            num_scalar_prefetch=2,
            grid=(chunks,),
            in_specs=[
                whole(half, rows, width),
                whole(half, rows, width),
                whole(chunks, 1, rows),
                pl.BlockSpec((1, lanes, rows), lambda i, o, q: (i, 0, 0)),
                pl.BlockSpec((1, 8, rows), lambda i, o, q: (i, 0, 0)),
                pl.BlockSpec((1, rows, lanes), lambda i, o, q: (q[i], 0, 0)),
            ],
            out_specs=[whole(half, rows, width)] * 2,
            scratch_shapes=[
                pltpu.VMEM((chunks, rows, lanes), BF),
                pltpu.VMEM((chunks, lanes, rows), BF),
                pltpu.VMEM((chunks, rows, lanes), BF),
                pltpu.VMEM((chunks, rows, lanes), BF),
                pltpu.VMEM((chunks, rows, 128), F32),
                pltpu.VMEM((chunks, rows, lanes), F32),
                pltpu.VMEM((chunks, rows, lanes), F32),
            ],
        ),
        compiler_params=pltpu.CompilerParams(vmem_limit_bytes=VMEM_LIMIT),
        cost_estimate=pl.CostEstimate(
            flops=pairs * rows * rows * 24000,
            bytes_accessed=chunks * rows * width * 8,
            transcendentals=pairs * rows * rows,
        ),
    )(meets, places, qkv_own, qkv_other, ids, flat, totals, grads)


def block_call(kernel, name, outs, tables, blocks, hbm, scratch, flops, space=pltpu.VMEM):
    moved = sum(x.size * x.dtype.itemsize for x in (*blocks, *hbm, *outs))
    return pl.pallas_call(
        kernel,
        name=name,
        out_shape=list(outs),
        in_specs=[pl.BlockSpec(memory_space=pltpu.SMEM)] * len(tables)
        + [pl.BlockSpec(memory_space=pltpu.VMEM)] * len(blocks)
        + [pl.BlockSpec(memory_space=pl.ANY)] * len(hbm),
        out_specs=[pl.BlockSpec(memory_space=space)] * len(outs),
        scratch_shapes=list(scratch),
        compiler_params=pltpu.CompilerParams(vmem_limit_bytes=VMEM_LIMIT),
        cost_estimate=pl.CostEstimate(flops=0, bytes_accessed=0, transcendentals=0),
    )(*tables, *blocks, *hbm)


def shaped(shape, dtype=BF):
    return jax.ShapeDtypeStruct(shape, dtype)


class Fetch:
    def __init__(self, table_ref, parts, columns, target, sems, at=0):
        self.table, self.parts, self.sems = table_ref, parts, sems
        self.source = pl.ds(*columns)
        self.target, self.place = target, pl.ds(at, columns[1])
        self.rows = parts[0].shape[1]
        self.count = target.shape[0] // self.rows

    def copy(self, part, piece, i):
        rows = pl.ds(pl.multiple_of(i * self.rows, self.rows), self.rows)
        return pltpu.make_async_copy(
            part.at[piece, :, self.source], self.target.at[rows, self.place], self.sems.at[i]
        )

    def start(self):
        def one(i, carry):
            index = self.table[i]
            first = 0
            for part in self.parts:
                count = part.shape[0]

                @pl.when((index >= first) & (index < first + count))
                def _():
                    self.copy(part, index - first, i).start()

                first += count
            return carry

        lax.fori_loop(0, self.count, one, 0)

    def wait(self):
        def one(i, carry):
            self.copy(self.parts[0], 0, i).wait()
            return carry

        lax.fori_loop(0, self.count, one, 0)


def row_blocks(rows, size=32):
    return [slice(r, r + size) for r in range(0, rows, size)]


def standardize(hidden):
    centered_input = hidden - jnp.mean(hidden, -1, keepdims=True)
    inverse_deviation = lax.rsqrt(
        jnp.mean(centered_input * centered_input, -1, keepdims=True) + NORM_EPS
    )
    return centered_input * inverse_deviation, inverse_deviation


def norm_backward(upstream_gradient, standardized_input, inverse_deviation, norm_gain):
    scaled_rows = upstream_gradient * norm_gain
    return inverse_deviation * (
        scaled_rows
        - jnp.mean(scaled_rows, -1, keepdims=True)
        - standardized_input * jnp.mean(scaled_rows * standardized_input, -1, keepdims=True)
    )


def out_norm(core, near_table, far_table, here, there, inputs, vectors, near_parts, far_part, first):
    groups, rows, lanes = here.shape
    half = D // 2
    chips = near_table.shape[0]

    def kernel(
        core_ref, near_ref, far_ref, here_ref, there_ref, input_ref, vector_ref, *refs
    ):
        parts, far_part_ref = refs[: len(near_parts)], refs[len(near_parts)]
        normed, standard, inverse, low, attended, matrix, branch, sems = refs[
            len(near_parts) + 1 :
        ]
        mine = pl.multiple_of(core_ref[0] * half, half)
        yours = pl.multiple_of((1 - core_ref[0]) * half, half)
        near = Fetch(near_ref, parts, (first, half), matrix, sems.at[0], mine)
        far = Fetch(far_ref, [far_part_ref], (0, half), matrix, sems.at[1], yours)
        near.start()
        far.start()
        for c in range(2):

            @pl.when(core_ref[0] == c)
            def _():
                for g in range(groups):
                    at = slice(c * half + g * lanes, c * half + (g + 1) * lanes)
                    attended[:, at] = here_ref[g]
                    at = slice((1 - c) * half + g * lanes, (1 - c) * half + (g + 1) * lanes)
                    attended[:, at] = there_ref[g]

        near.wait()
        far.wait()
        for n in range(0, D, 256):
            branch[:, n : n + 256] = nn(attended[...], matrix[:, n : n + 256])
        bias, gain, shift = vector_ref[2:3], vector_ref[3:4], vector_ref[4:5]
        for at in row_blocks(rows):
            hidden = input_ref[at].astype(F32) + branch[at] + bias
            standardized, deviation = standardize(hidden)
            result = standardized * gain + shift
            normed[at] = result
            standard[at] = standardized
            inverse[at] = jnp.broadcast_to(deviation, (32, 128))
            low[at] = result.astype(BF)

    return block_call(
        kernel,
        "out_norm",
        [
            shaped((rows, D), F32),
            shaped((rows, D), F32),
            shaped((rows, 128), F32),
            shaped((rows, D)),
            shaped((rows, D)),
            shaped((D, D)),
        ],
        [core, near_table, far_table],
        [here, there, inputs, vectors],
        [*near_parts, far_part],
        [pltpu.VMEM((rows, D), F32), pltpu.SemaphoreType.DMA((2, chips))],
        2 * rows * D * D,
    )


def feed_forward(table, back_table, low_own, low_other, bias, in_parts, back_parts):
    rows = low_own.shape[0]
    units = bias.shape[1]
    chips = table.shape[0]
    tile = 256

    def kernel(table_ref, back_ref, own_ref, other_ref, bias_ref, *refs):
        n = len(in_parts)
        parts, back, refs = refs[:n], refs[n : 2 * n], refs[2 * n :]
        fed_own, fed_other, active, slope, low, in_mat, back_here, sems = refs
        first = Fetch(table_ref, parts, (0, units), in_mat, sems.at[0])
        second = Fetch(back_ref, back, (0, D), back_here, sems.at[1])
        first.start()
        low[:rows] = own_ref[...]
        low[rows:] = other_ref[...]
        first.wait()
        second.start()
        for t in range(0, units, tile):
            at = slice(t, t + tile)
            inner = nn(low[...], in_mat[:, at]) + bias_ref[:, at]
            share = 0.5 + 0.5 * lax.erf(inner * (0.5**0.5))
            active[:, at] = (inner * share).astype(BF)
            bell = jnp.exp(inner * inner * -0.5) * (1.0 / (2.0 * np.pi) ** 0.5)
            slope[:, at] = (share + inner * bell).astype(BF)
        second.wait()
        for n in range(0, D, tile):
            at = slice(n, n + tile)
            fed = nn(active[...], back_here[:, at])
            fed_own[:, at] = fed[:rows]
            fed_other[:, at] = fed[rows:].astype(BF)

    return block_call(
        kernel,
        "feed_forward",
        [
            shaped((rows, D), F32),
            shaped((rows, D)),
            shaped((2 * rows, units)),
            shaped((2 * rows, units)),
        ],
        [table, back_table],
        [low_own, low_other, bias],
        [*in_parts, *back_parts],
        [
            pltpu.VMEM((2 * rows, D), BF),
            pltpu.VMEM((D, units), BF),
            pltpu.VMEM((units, D), BF),
            pltpu.SemaphoreType.DMA((2, chips)),
        ],
        8 * rows * D * units,
    )


def last_norm(normed, fed_own, fed_there, vectors, cotangent):
    rows = normed.shape[0]

    def kernel(normed_ref, own_ref, there_ref, vector_ref, up_ref, result, grad, low, sums):
        bias, gain, shift = vector_ref[5:6], vector_ref[6:7], vector_ref[7:8]
        totals = [jnp.zeros((8, D), F32) for _ in range(3)]
        for at in row_blocks(rows):
            hidden = normed_ref[at] + own_ref[at] + there_ref[at].astype(F32) + bias
            standardized, deviation = standardize(hidden)
            result[at] = (standardized * gain + shift).astype(BF)
            up = up_ref[at].astype(F32)
            down = norm_backward(up, standardized, deviation, gain)
            grad[at] = down
            down_low = down.astype(BF)
            low[at] = down_low
            for n, term in enumerate((up * standardized, up, down_low.astype(F32))):
                totals[n] = totals[n] + fold(term, jnp.add)
        sums[...] = jnp.concatenate(
            [jnp.sum(total, 0, keepdims=True) for total in totals] + [jnp.zeros((5, D), F32)],
            axis=0,
        )

    return block_call(
        kernel,
        "last_norm",
        [shaped((rows, D)), shaped((rows, D), F32), shaped((rows, D)), shaped((8, D), F32)],
        [],
        [normed, fed_own, fed_there, vectors, cotangent],
        [],
        [],
        64 * rows * D,
    )


def place_pieces(value, first, rows, table_ref, stack, columns, at_row=0):
    for q in range(value.shape[0] // rows):
        piece = value[q * rows : (q + 1) * rows].astype(BF)
        stack[table_ref[first + q], at_row : at_row + rows, columns] = piece


def split_pieces(stack, keep, away, sems):
    half = keep.shape[0]
    copies = [
        pltpu.make_async_copy(stack.at[pl.ds(n * half, half)], out, sems.at[n])
        for n, out in enumerate((keep, away))
    ]
    for copy in copies:
        copy.start()
    for copy in copies:
        copy.wait()


def pieces_scratch(count, rows, columns):
    return [pltpu.VMEM((count, rows, columns), BF), pltpu.SemaphoreType.DMA((2,))]


def grad_back(table, active, up_own, up_other):
    rows = up_own.shape[0]
    units = active.shape[1]
    chips = table.shape[0]
    part = units // chips
    tile = 256

    def kernel(table_ref, active_ref, own_ref, other_ref, keep, away, stack, sems, up):
        up[:rows] = own_ref[...]
        up[rows:] = other_ref[...]
        for t in range(0, units, tile):
            value = tn(active_ref[:, t : t + tile], up[...])
            place_pieces(value, t // part, part, table_ref, stack, slice(0, D))
        split_pieces(stack, keep, away, sems)

    return block_call(
        kernel,
        "grad_back",
        [shaped((chips // 2, part, D))] * 2,
        [table],
        [active, up_own, up_other],
        [],
        [*pieces_scratch(chips, part, D), pltpu.VMEM((2 * rows, D), BF)],
        4 * rows * units * D,
        pl.ANY,
    )


def feed_backward(table, back_table, up_own, up_other, slope, in_parts, back_parts):
    rows = up_own.shape[0]
    units = slope.shape[1]
    chips = table.shape[0]
    tile = 256

    def kernel(table_ref, back_ref, own_ref, other_ref, slope_ref, *refs):
        n = len(in_parts)
        parts, back, refs = refs[:n], refs[n : 2 * n], refs[2 * n :]
        down_own, down_other, grad_inner, bias, up, in_mat, back_here, sems = refs
        first = Fetch(table_ref, parts, (0, units), in_mat, sems.at[0])
        second = Fetch(back_ref, back, (0, D), back_here, sems.at[1])
        second.start()
        up[:rows] = own_ref[...]
        up[rows:] = other_ref[...]
        second.wait()
        first.start()
        for t in range(0, units, tile):
            at = slice(t, t + tile)
            inner = (nt(up[...], back_here[at]) * slope_ref[:, at].astype(F32)).astype(BF)
            grad_inner[:, at] = inner
            bias[:, at] = jnp.sum(fold(inner.astype(F32), jnp.add), 0, keepdims=True)
        first.wait()
        for n in range(0, D, tile):
            at = slice(n, n + tile)
            down = nt(grad_inner[...], in_mat[at])
            down_own[:, at] = down[:rows]
            down_other[:, at] = down[rows:].astype(BF)

    return block_call(
        kernel,
        "feed_backward",
        [
            shaped((rows, D), F32),
            shaped((rows, D)),
            shaped((2 * rows, units)),
            shaped((1, units), F32),
        ],
        [table, back_table],
        [up_own, up_other, slope],
        [*in_parts, *back_parts],
        [
            pltpu.VMEM((2 * rows, D), BF),
            pltpu.VMEM((D, units), BF),
            pltpu.VMEM((units, D), BF),
            pltpu.SemaphoreType.DMA((2, chips)),
        ],
        8 * rows * D * units,
    )


def out_norm_backward(
    core, grad_two, down_own, down_there, standard, inverse, vectors, attended, matrix
):
    rows = grad_two.shape[0]
    half = D // 2
    lanes = 128 if half % 128 == 0 else half

    def kernel(
        core_ref,
        two_ref,
        own_ref,
        there_ref,
        standard_ref,
        inverse_ref,
        vector_ref,
        attended_ref,
        matrix_ref,
        grad_one,
        low,
        sums,
        grad_heads,
        grad_far,
    ):
        gain = vector_ref[3:4]
        totals = [jnp.zeros((8, D), F32) for _ in range(3)]
        for at in row_blocks(rows):
            grad = two_ref[at] + own_ref[at] + there_ref[at].astype(F32)
            standardized = standard_ref[at]
            down = norm_backward(grad, standardized, inverse_ref[at, :1], gain)
            grad_one[at] = down
            down_low = down.astype(BF)
            low[at] = down_low
            for n, term in enumerate((grad * standardized, grad, down_low.astype(F32))):
                totals[n] = totals[n] + fold(term, jnp.add)
        sums[...] = jnp.concatenate(
            [jnp.sum(total, 0, keepdims=True) for total in totals] + [jnp.zeros((5, D), F32)],
            axis=0,
        )
        for n in range(0, D, 256):
            grad_heads[:, n : n + 256] = nt(low[...], matrix_ref[n : n + 256]).astype(BF)
        yours = pl.ds(pl.multiple_of((1 - core_ref[0]) * half, half), half)
        for n in range(0, D, 256):
            grad_far[n : n + 256] = tn(attended_ref[:, n : n + 256], low[:, yours]).astype(BF)

    return block_call(
        kernel,
        "out_norm_backward",
        [
            shaped((rows, D), F32),
            shaped((rows, D)),
            shaped((8, D), F32),
            shaped((rows, D)),
            shaped((D, half)),
        ],
        [core],
        [grad_two, down_own, down_there, standard, inverse, vectors, attended, matrix],
        [],
        [],
        3 * rows * D * D,
    )


def grad_in_out(core, table, low_own, low_other, grad_inner, attended, low_grad, far):
    rows = low_own.shape[0]
    units = grad_inner.shape[1]
    chips = table.shape[0]
    shard = D // chips
    half = D // 2
    tile = 256

    def kernel(
        core_ref,
        table_ref,
        own_ref,
        other_ref,
        inner_ref,
        attended_ref,
        grad_ref,
        far_ref,
        keep,
        away,
        stack,
        sems,
        low,
    ):
        low[:rows] = own_ref[...]
        low[rows:] = other_ref[...]
        mine = pl.ds(pl.multiple_of(core_ref[0] * half, half), half)
        for t in range(0, D, tile):
            at = slice(t, t + tile)
            value = tn(low[:, at], inner_ref[...])
            place_pieces(value, t // shard, shard, table_ref, stack, slice(0, units))
            value = tn(attended_ref[:, at], grad_ref[:, mine]) + far_ref[at].astype(F32)
            place_pieces(value, t // shard, shard, table_ref, stack, slice(units, units + half))
        split_pieces(stack, keep, away, sems)

    return block_call(
        kernel,
        "grad_in_out",
        [shaped((chips // 2, shard, units + half))] * 2,
        [core, table],
        [low_own, low_other, grad_inner, attended, low_grad, far],
        [],
        [*pieces_scratch(chips, shard, units + half), pltpu.VMEM((2 * rows, D), BF)],
        5 * rows * units * D,
        pl.ANY,
    )


def grad_projections(
    numbers, table, tokens_own, tokens_other, down_own, down_other, sums_one, sums_two, in_bias, extra
):
    half, rows, width = down_own.shape
    lanes = width // 3
    chips = table.shape[0]
    shard = D // chips
    units = in_bias.shape[1]
    part = units // chips
    tile = 256

    def kernel(
        number_ref,
        table_ref,
        x_own,
        x_other,
        own_ref,
        other_ref,
        one_ref,
        two_ref,
        bias_ref,
        keep,
        away,
        stack,
        sems,
    ):
        own = own_ref[...].reshape(half * rows, width)
        other = other_ref[...].reshape(half * rows, width)
        for t in range(0, D, tile):
            value = jnp.zeros((tile, width), F32)
            for p in range(half):
                value = value + tn(x_own[p, :, t : t + tile], own_ref[p])
                value = value + tn(x_other[p, :, t : t + tile], other_ref[p])
            place_pieces(value, t // shard, shard, table_ref, stack, slice(0, width))
        totals = jnp.sum(
            fold(own.astype(F32), jnp.add) + fold(other.astype(F32), jnp.add),
            0,
            keepdims=True,
        )
        pair = jnp.concatenate([totals[:, :lanes], totals[:, 2 * lanes :]], axis=0)
        pair = jnp.concatenate(
            [jnp.where(number_ref[1] == a, pair, 0.0) for a in range(D // lanes)], axis=1
        )
        one, two = one_ref[...], two_ref[...]
        stacked = jnp.concatenate(
            [pair, one[2:3], one[0:1], one[1:2], two[2:3], two[0:1], two[1:2]], axis=0
        )
        blank = jnp.zeros((1, part), F32)
        for i in range(chips):
            bias = bias_ref[:, i * part : (i + 1) * part]
            bias = jnp.where(
                number_ref[0] == 0,
                jnp.concatenate([bias, blank], axis=1),
                jnp.concatenate([blank, bias], axis=1),
            )
            top = stacked[:, i * shard : (i + 1) * shard]
            rest = extra - 9
            block = jnp.concatenate(
                [
                    jnp.concatenate([top, jnp.zeros((8, width - shard), F32)], axis=1),
                    jnp.concatenate([bias, jnp.zeros((1, width - 2 * part), F32)], axis=1),
                    jnp.zeros((rest, width), F32),
                ],
                axis=0,
            )
            place_pieces(block, i, extra, table_ref, stack, slice(0, width), shard)
        split_pieces(stack, keep, away, sems)

    return block_call(
        kernel,
        "grad_projections",
        [shaped((chips // 2, shard + extra, width))] * 2,
        [numbers, table],
        [
            tokens_own,
            tokens_other,
            down_own,
            down_other,
            sums_one,
            sums_two,
            in_bias,
        ],
        [],
        pieces_scratch(chips, shard + extra, width),
        4 * half * rows * D * width,
        pl.ANY,
    )


def pack(numbers, weights, vectors, bias, marks, groups, extra):
    shard = weights[0].shape[0]
    half = D // 2
    lanes = half // groups
    width = 3 * lanes

    def kernel(number_ref, *refs):
        *weight_refs, vector_ref, bias_ref, mark_ref, out = refs

        def lines(row):
            count = -(-row.shape[1] // width)
            padded = jnp.concatenate(
                [row, jnp.zeros((1, count * width - row.shape[1]), F32)], axis=1
            )
            return [padded[:, n * width : (n + 1) * width] for n in range(count)]

        small = vector_ref[...].astype(F32)
        block = [jnp.concatenate([small, jnp.zeros((8, width - small.shape[1]), F32)], axis=1)]
        block += lines(bias_ref[...].astype(F32)) + lines(mark_ref[...].astype(F32))
        filled = 8 + len(block) - 1
        block = jnp.concatenate(block + [jnp.zeros((extra - filled, width), F32)], axis=0)
        block = block.astype(BF)
        for d in range(groups):
            out[d, shard:] = block
        for c in range(2):

            @pl.when(number_ref[0] == c)
            def _():
                for a in range(groups):
                    place = number_ref[2 + a]
                    for n, weight in enumerate(weight_refs):
                        start = c * half + a * lanes
                        out[place, :shard, n * lanes : (n + 1) * lanes] = weight[
                            :, start : start + lanes
                        ]

    return block_call(
        kernel,
        "pack",
        [shaped((groups, shard + extra, width))],
        [numbers],
        [*weights, vectors, bias, marks],
        [],
        [],
        0,
    )[0]


def send(value, perm):
    return lax.ppermute(value, AXES, perm)


def gather_stages(block, perms):
    for perm in perms[:-1]:
        block = jnp.concatenate([block, send(block, perm)], axis=0)
    return [block, send(block, perms[-1])]


def hold(value, *earlier):
    return lax.optimization_barrier((value, *earlier))[0]


class Gather:
    def __init__(self, block, perms):
        self.parts, self.perms = [block], perms

    def stage(self, *earlier):
        first = hold(self.parts[0], *earlier) if earlier else self.parts[0]
        block = jnp.concatenate([first, *self.parts[1:]], axis=0)
        self.parts = [block, send(block, self.perms[0])]
        self.perms = self.perms[1:]
        return self.parts[1]


class Scatter:
    def __init__(self, keep, away, perms):
        self.keep, self.away, self.perms = keep, away, perms[::-1]

    def stage(self, *earlier):
        arrived = send(self.away, self.perms[0])
        arrived = hold(arrived, *earlier) if earlier else arrived
        self.perms = self.perms[1:]
        if self.perms:
            half = self.keep.shape[0] // 2
            self.away = self.keep[half:] + arrived[half:]
            self.keep = self.keep[:half] + arrived[:half]
        else:
            self.keep = self.keep.astype(F32) + arrived.astype(F32)
        return arrived

    def finish(self):
        while self.perms:
            self.stage()
        return self.keep


def pieces(count, rows, columns):
    return jax.ShapeDtypeStruct((count, rows, columns), BF)


def body(
    plan,
    tokens,
    segment_ids,
    w_query,
    b_query,
    w_key,
    w_value,
    b_value,
    w_out,
    b_out,
    g_attn,
    n_attn,
    w_in,
    b_in,
    w_back,
    b_back,
    g_ffn,
    n_ffn,
    cotangent,
):
    chips, groups, heads, ctx = plan.chips, plan.groups, plan.heads, plan.ctx
    core = lax.axis_index("dp")
    place = lax.axis_index("ctx")
    device = (core * ctx + place) * plan.fsdp + lax.axis_index("fsdp")
    side, group = place // groups, place % groups
    rows = tokens.shape[1]
    shard = w_query.shape[0]
    hidden = w_back.shape[0]
    part = hidden // 2
    units = FF // 2
    lanes = heads * HD
    half_d = D // 2
    width = 3 * lanes
    bias_rows, mark_rows = -(-hidden // width), -(-rows // width)
    extra = 16 * (-(-(8 + bias_rows + mark_rows) // 16))
    swap = plan.core_swap()
    in_perms = plan.chip_perms(plan.in_orders)
    back_perms = plan.chip_perms(plan.back_orders)

    side_table = plan.side_pieces()
    tables = dict(
        w_in=plan.chip_gather(plan.in_orders),
        far=plan.other_core(plan.chip_gather(plan.in_orders)),
        w_back=plan.chip_gather(plan.back_orders),
        pieces=invert(side_table),
        chunks=plan.table(lambda c, j, f: [plan.chunk_of(c, j, p) for p in range(ctx)]),
        numbers=plan.table(
            lambda c, j, f: [c, c * groups + j % groups]
            + [a ^ (j % groups) for a in range(groups)]
        ),
    )
    table_row = lax.dynamic_index_in_dim(
        jnp.asarray(np.concatenate(list(tables.values()), axis=1)), device, 0, False
    )
    starts = np.cumsum([0] + [t.shape[1] for t in tables.values()])
    look = {
        name: table_row[starts[n] : starts[n + 1]] for n, name in enumerate(tables)
    }

    def mine(columns, size, axis=1):
        return lax.dynamic_slice_in_dim(columns, core * size, size, axis)

    w_in_mine = lax.dynamic_index_in_dim(
        w_in.reshape(shard, chips, 2, part), core, 2, False
    ).reshape(shard, units)
    w_in_mine = jnp.concatenate([w_in_mine, mine(w_out, half_d)], axis=1)[None]
    w_back_mine = mine(w_back, part, 0)[None]
    in_gather = Gather(w_in_mine, in_perms)
    back_gather = Gather(w_back_mine, back_perms)

    inputs = tokens[0]
    turned = send(inputs, plan.turn())
    block = turned[None]
    reached = [turned]
    for perm in plan.group_perms():
        reached.append(send(block, perm))
        block = jnp.concatenate([block, reached[-1]], axis=0)
    tokens_own = block
    tokens_other = send(tokens_own, swap)
    in_gather.stage(turned)
    in_gather.stage(reached[1])
    back_gather.stage(reached[1])
    in_gather.stage(reached[2])
    back_gather.stage(reached[2])

    vectors = jnp.stack([b_query, b_value, b_out, g_attn, n_attn, b_back, g_ffn, n_ffn])
    messages = pack(
        look["numbers"],
        [w_query, w_key, w_value],
        vectors,
        b_in[None],
        segment_ids,
        groups,
        extra,
    )
    arrived = [messages[0]] + [
        send(messages[d], plan.group_direct(d)) for d in range(1, groups)
    ]
    gathered = gather_stages(hold(jnp.stack(arrived), reached[1]), plan.side_perms())
    heads_mat, extras = route(
        gathered,
        look["pieces"],
        [pieces(chips, shard, width), pieces(chips, extra, width)],
        [((0, 1), i, 0, shard, 0, i, 0) for i in range(chips)]
        + [((0, 1), i, shard, extra, 1, i, 0) for i in range(chips)],
    )
    heads_mat = heads_mat.reshape(D, width)
    vectors = extras[:, :8, :shard].transpose(1, 0, 2).reshape(8, D).astype(F32)
    in_bias = extras[:, 8 : 8 + bias_rows].reshape(chips, -1)[:, :hidden]
    in_bias = (
        lax.dynamic_slice_in_dim(in_bias, core * part, part, 1).reshape(1, units).astype(F32)
    )
    at = 8 + bias_rows
    ids_here = extras[:, at : at + mark_rows].reshape(chips, -1)[:, :rows]
    ids_here = lax.dynamic_index_in_dim(
        ids_here.reshape(ctx, plan.fsdp, rows), lax.axis_index("fsdp"), 1, False
    )
    ids_there = send(ids_here, swap)
    ids_all = jnp.where(core == side, ids_here, ids_there).astype(F32)
    chosen = look["chunks"][:, None] == jnp.arange(ctx)[None]
    ids = jnp.sum(jnp.where(chosen[:, :, None], ids_all[None], 0.0), axis=1)
    first, last = ids[:, 0], ids[:, -1]
    overlap = ((first[:, None] <= last[None]) & (first[None] <= last[:, None])).astype(jnp.int32)
    ids = ids[:, None, :]
    meets = listing(overlap)

    start = core * half_d + group * lanes
    heads_bias = jnp.concatenate(
        [
            lax.dynamic_slice(vectors, (0, start), (1, lanes)),
            jnp.zeros((1, lanes), F32),
            lax.dynamic_slice(vectors, (1, start), (1, lanes)),
        ],
        axis=1,
    )

    def project(block):
        return (
            jnp.einsum("ptd,dw->ptw", block, heads_mat, preferred_element_type=F32) + heads_bias
        ).astype(BF)

    qkv_own, qkv_other = project(tokens_own), project(tokens_other)
    in_gather.stage(qkv_own)
    in_parts = in_gather.parts
    back_gather.stage(qkv_own)
    qkv_other = hold(qkv_other, in_parts[0], back_gather.parts[0])
    sent, flat, totals = attend_forward(
        look["chunks"], qkv_own, qkv_other, ids, meets, heads
    )
    met = lax.all_to_all(sent, "ctx", 0, 0, tiled=True).reshape(2, groups, rows, lanes)
    back_gather.stage(met, in_parts[1])
    back_parts = back_gather.parts
    out_there = jnp.concatenate([part[:, :, units:] for part in in_parts], axis=0)
    out_there = send(out_there, swap)
    here = lax.dynamic_index_in_dim(met, core, 0, False)
    there = send(lax.dynamic_index_in_dim(met, 1 - core, 0, False), swap)

    core_number = look["numbers"][:1]
    normed, standard, inverse, low_own, attended, out_mat = out_norm(
        core_number,
        look["w_in"],
        look["far"],
        here,
        there,
        inputs,
        vectors,
        in_parts,
        out_there,
        units,
    )
    low_other = send(low_own, swap)
    fed_own, fed_other, active, slope = feed_forward(
        look["w_in"], look["w_back"], low_own, low_other, in_bias, in_parts, back_parts
    )
    result, grad_two, up_own, sums_two = last_norm(
        normed, fed_own, send(fed_other, swap), vectors, cotangent[0]
    )
    up_other = send(up_own, swap)
    down_own, down_other, grad_inner, grad_in_bias = feed_backward(
        look["w_in"],
        look["w_back"],
        up_own,
        up_other,
        slope,
        in_parts,
        back_parts,
    )
    grad_one, low_grad, sums_one, grad_heads, grad_far = out_norm_backward(
        core_number,
        grad_two,
        down_own,
        send(down_other, swap),
        standard,
        inverse,
        vectors,
        attended,
        out_mat,
    )
    grad_heads = grad_heads.reshape(rows, 2, groups, lanes).transpose(1, 2, 0, 3)
    kept = lax.dynamic_index_in_dim(grad_heads, core, 0, False)
    towards = send(lax.dynamic_index_in_dim(grad_heads, 1 - core, 0, False), swap)
    grad_heads = jnp.where(
        core == 0, jnp.stack([kept, towards]), jnp.stack([towards, kept])
    ).reshape(ctx, rows, lanes)
    grads = lax.all_to_all(grad_heads, "ctx", 0, 0, tiled=True)
    back_scatter = Scatter(
        *grad_back(look["w_back"], hold(active, grad_heads), up_own, up_other), back_perms
    )
    in_scatter = Scatter(
        *grad_in_out(
            core_number,
            look["w_in"],
            low_own,
            low_other,
            hold(grad_inner, back_scatter.away),
            attended,
            low_grad,
            send(grad_far, swap),
        ),
        in_perms,
    )

    grads = hold(grads, in_scatter.away)
    back_first = back_scatter.stage()
    in_first = in_scatter.stage()
    qkv_grads = attend_backward(
        look["chunks"], qkv_own, qkv_other, ids, meets, grads, flat, totals, heads
    )
    qkv_grads = lax.optimization_barrier((*qkv_grads, back_first))[:2]
    down_own, down_other = qkv_grads

    def back_project(down):
        return jnp.einsum("ptw,dw->ptd", down, heads_mat, preferred_element_type=F32)

    towards = send(back_project(down_other).astype(BF), swap)
    block = (back_project(down_own) + towards.astype(F32)).astype(BF)
    whole_block = block
    down_own, down_other, _ = lax.optimization_barrier((down_own, down_other, block))
    side_scatter = Scatter(
        *grad_projections(
            look["numbers"],
            look["pieces"],
            tokens_own,
            tokens_other,
            down_own,
            down_other,
            sums_one,
            sums_two,
            grad_in_bias,
            extra,
        ),
        plan.side_perms(),
    )
    reached = []
    for perm in plan.group_perms()[::-1]:
        half = block.shape[0] // 2
        reached.append(send(block[half:], perm))
        block = block[:half] + reached[-1]
    in_scatter.stage(whole_block)
    back_scatter.stage(whole_block)
    in_scatter.stage(reached[0])
    side_scatter.stage(reached[0])
    in_away = in_scatter.away
    back_scatter.stage(reached[1])
    ended = send(hold(block[0], in_away), plan.turn())
    side_last = send(side_scatter.away, side_scatter.perms[0])
    low_by_group = (side_scatter.keep + hold(side_last, reached[1]))
    back_last = back_scatter.finish()
    grad_back_mat = hold(back_last[0], reached[1])
    grad_inputs = grad_one + ended.astype(F32)
    in_last = in_scatter.finish()
    in_scatter.keep = hold(in_last, reached[1])
    by_group = [low_by_group[0]] + [
        send(low_by_group[d], plan.group_direct(d)) for d in range(1, groups)
    ]
    by_group = jnp.stack(by_group).astype(F32)
    grad_extras = jnp.sum(by_group[:, shard:], 0)
    grad_columns = jnp.stack(
        [lax.dynamic_index_in_dim(by_group, group ^ d, 0, False)[:shard] for d in range(groups)]
    )
    grad_columns = grad_columns.reshape(groups, shard, 3, lanes).transpose(2, 1, 0, 3)
    grad_columns = grad_columns.reshape(3, shard, half_d)
    grad_in_mat = in_scatter.finish()[0]
    grad_out_mat = grad_in_mat[:, units:]
    grad_in_mat = grad_in_mat[:, :units]

    def both(half, axis):
        half = half.astype(BF)
        there = send(half, swap)
        return jnp.where(
            core == 0, jnp.stack([half, there], axis=axis), jnp.stack([there, half], axis=axis)
        ).astype(F32)

    grad_columns = both(grad_columns, 2).reshape(3, shard, D)
    grad_out_mat = both(grad_out_mat, 1).reshape(shard, D)
    grad_in_mat = both(grad_in_mat.reshape(shard, chips, part), 2).reshape(
        shard, FF
    )
    grad_back_mat = both(grad_back_mat, 0).reshape(hidden, D)
    sums = grad_extras + send(grad_extras, swap)
    small = [sums[which, :shard] for which in range(8)]
    return (
        result[None],
        grad_inputs[None],
        grad_columns[0],
        small[0],
        grad_columns[1],
        grad_columns[2],
        small[1],
        grad_out_mat,
        small[2],
        small[3],
        small[4],
        grad_in_mat,
        sums[8:].reshape(-1)[:hidden],
        grad_back_mat,
        small[5],
        small[6],
        small[7],
    )


def solution(mesh):
    owned = ("ctx", "fsdp")
    matrix, vector = P(owned, None), P(owned)
    sequence = P(("dp", "fsdp"), "ctx", None)
    return jax.shard_map(
        partial(body, Plan(mesh)),
        mesh=mesh,
        in_specs=(
            sequence,
            P(("dp", "fsdp"), "ctx"),
            matrix,
            vector,
            matrix,
            matrix,
            vector,
            matrix,
            vector,
            vector,
            vector,
            matrix,
            vector,
            matrix,
            vector,
            vector,
            vector,
            sequence,
        ),
        out_specs=(
            sequence,
            sequence,
            matrix,
            vector,
            matrix,
            matrix,
            vector,
            matrix,
            vector,
            vector,
            vector,
            matrix,
            vector,
            matrix,
            vector,
            vector,
            vector,
        ),
        check_vma=False,
    )
```
